256 devices in a mesh: scene: 32 (over z, x), seq: 8 (over y, core).
Axes of the slice: x: 4, y: 4, z: 8, core: 2. Of those that a mesh axis runs over, the one named last changes fastest.
Arguments:
- x_in: bfloat16 [262144, 256], P(('scene', 'seq')), may hold values from -6 to 6
- counts: int32 [32], P('scene'), may hold values from 1024 to 8192, as said below
- ln_gains: float32 [2, 256], replicated, may hold values from 0.5 to 1.5
- w_qkv: bfloat16 [2, 256, 768], replicated
- w_proj: bfloat16 [2, 256, 256], replicated, may hold values from -0.375 to 0.375
- cotangent: bfloat16 [262144, 256], P(('scene', 'seq')), may hold values from -24 to 24
Outputs:
- result_out: bfloat16 [262144, 256], P(('scene', 'seq'))
- grad_input: bfloat16 [262144, 256], P(('scene', 'seq'))
- grad_gains: float32 [2, 256], replicated
- grad_qkv: float32 [2, 256, 768], replicated
- grad_proj: float32 [2, 256, 256], replicated
The draws below stay inside these ranges and needn't reach their ends.
Inputs may be any that keep to these rules, and one draw needn't show every extreme that they name: `counts`: some scene has all 8192 slots occupied.
All inputs are finite; a program needn't handle non-finite values.
Results may differ from the reference program's by a relative error of at most 0.034.
Values may be sent and summed in bfloat16 or wider, within the bound.
No kernel may reach another device: no remote copies, remote signals or barrier semaphores. Data moves between devices by JAX's collectives and lax.ppermute only.
A program may use at most 128 MiB of HBM per device.

```python
import jax
import jax.numpy as jnp
from jax import lax

C = 256
HEADS = 8
WIN = 1024
SCENE_TOK = 8192
SCENES = 32
TOKENS = 262144
N_SEQ = 8


def draw_counts(key, part):
    base_counts = jax.random.randint(key, (SCENES,), SCENE_TOK // 8, SCENE_TOK + 1)
    chosen = jax.random.randint(jax.random.fold_in(key, 7), (), 0, SCENES)
    return jnp.where(jnp.arange(SCENES) == chosen, SCENE_TOK, base_counts).astype(jnp.int32)


def draw_w_qkv(key, part):
    base_draw = jax.random.normal(key, (2, C, 3 * C), jnp.float32) * C ** (-0.5)
    return base_draw.astype(jnp.bfloat16)


def raised(drawn, key, source, target, parts, factor):
    owner, partner = [(jnp.arange(drawn.shape[dim]) // (drawn.shape[dim] // parts)).reshape([-1 if axis == dim else 1 for axis in range(drawn.ndim)]) for dim in (source, target)]
    chosen = jax.random.permutation(key, parts)[partner]
    strong = (owner == chosen) | (owner == (partner + parts // 2) % parts)
    return jnp.where(strong, factor * drawn, drawn)


def shard_levels(own_key, dims, split, smallest, high):
    def one(dim, blocks):
        steps = jax.random.uniform(jax.random.fold_in(jax.random.fold_in(own_key, 6), dim), (blocks,), jnp.float32, smallest / len(split), high / len(split))
        return jnp.repeat(jnp.exp(steps), dims[dim] // blocks).reshape((-1,) + (1,) * (len(dims) - dim - 1))

    loudness = one(*split[0])
    for cut in split[1:]:
        loudness = loudness * one(*cut)
    return loudness


def gaussian(stream_key, dims, scale, bound, cuts=(), kind=jnp.bfloat16):
    result = jax.random.normal(stream_key, dims, jnp.float32) * scale
    if len(cuts) > 0:
        result = shard_levels(stream_key, dims, cuts, -0.22, 0.18) * result
    return jnp.clip(result, min=-bound, max=bound).astype(kind)


def gaussian_with(key, dims, deviation, most, split, heavy, held_as=jnp.bfloat16):
    drawn = deviation * jax.random.normal(key, dims, jnp.float32)
    if split:
        drawn = drawn * shard_levels(key, dims, split, -0.22, 0.18)
    return jnp.clip(raised(drawn, jax.random.fold_in(key, 3), *heavy), -most, most).astype(held_as)


def setup_inputs(seed: int = 0) -> dict:
    splits = jax.random.split(jax.random.key(seed), 7)
    return {
        "x_in": gaussian(splits[0], (TOKENS, C), 1.0, 6.0, ((0, 256),)),
        "counts": draw_counts(jax.random.fold_in(splits[6], 71), 0),
        "ln_gains": jnp.clip(1.0 + 0.1 * jax.random.normal(splits[2], (2, C), jnp.float32), 0.5, 1.5),
        "w_qkv": draw_w_qkv(jax.random.fold_in(splits[6], 71), 0),
        "w_proj": gaussian(splits[4], (2, C, C), C ** -0.5, 0.375),
        "cotangent": gaussian_with(splits[5], (TOKENS, C), 1.0, 24.0, ((0, 256),), (0, 1, 256, 6.0)),
    }


EPSILON = 1e-05
MASKED = -1e+30

def layer_norm(inputs, gain_vec):
    average = lax.optimization_barrier(jnp.mean(inputs, axis=-1, keepdims=True))
    centred = inputs - average
    spread = lax.optimization_barrier(jnp.mean(centred * centred, axis=-1, keepdims=True))
    return centred * lax.rsqrt(spread + EPSILON) * gain_vec

def head_attend(queries, keys_part, values, same_group):
    scores = jnp.dot(queries, keys_part.T, preferred_element_type=jnp.float32) * queries.shape[1] ** (-0.5)
    scores = jnp.where(same_group, scores, MASKED)
    largest = lax.optimization_barrier(jnp.max(scores, axis=1, keepdims=True))
    weights = jnp.exp(scores - largest)
    row_total = lax.optimization_barrier(jnp.sum(weights, axis=1, keepdims=True))
    weights_bf = (weights / row_total).astype(jnp.bfloat16)
    return jnp.dot(weights_bf, values, preferred_element_type=jnp.float32).astype(jnp.bfloat16)

def window_attend(packed, valid_win):
    length = packed.shape[0]
    feature = packed.shape[1] // 3
    split_heads = packed.reshape(length, 3, HEADS, feature // HEADS).transpose(1, 2, 0, 3)
    same_group = valid_win[:, None] == valid_win[None, :]
    checked = jax.checkpoint(head_attend)

    def one_head(triple):
        return checked(triple[0], triple[1], triple[2], same_group)
    mixed_heads = lax.map(one_head, (split_heads[0], split_heads[1], split_heads[2]))
    return mixed_heads.transpose(1, 0, 2).reshape(length, feature)

def attend(packed, valid_rows):
    row_count = packed.shape[0]
    windows = row_count // WIN

    def one_window(pair_in):
        return window_attend(pair_in[0], pair_in[1])
    mixed_win = lax.map(one_window, (packed.reshape(windows, WIN, packed.shape[1]), valid_rows.reshape(windows, WIN)))
    return mixed_win.reshape(row_count, packed.shape[1] // 3)

def attend_back(packed, valid_rows, d_mixed):
    row_count = packed.shape[0]
    windows = row_count // WIN
    feature = packed.shape[1] // 3

    def one_window(triple):

        def forward_win(block_in):
            return window_attend(block_in, triple[1])
        _, pull_back = jax.vjp(forward_win, triple[0])
        return pull_back(triple[2])[0]
    grads = lax.map(one_window, (packed.reshape(windows, WIN, 3 * feature), valid_rows.reshape(windows, WIN), d_mixed.reshape(windows, WIN, feature)))
    return grads.reshape(row_count, 3 * feature)

def block_forward(inputs, valid_rows, gain_vec, w_mix, w_out):
    normed = layer_norm(inputs.astype(jnp.float32), gain_vec).astype(jnp.bfloat16)
    packed = jnp.dot(normed, w_mix, preferred_element_type=jnp.float32).astype(jnp.bfloat16)
    mixed_rows = attend(packed, valid_rows)
    outputs = (inputs.astype(jnp.float32) + jnp.dot(mixed_rows, w_out, preferred_element_type=jnp.float32)).astype(jnp.bfloat16)
    return (outputs, (normed, packed, mixed_rows))

def finish_back(inputs, gain_vec, w_mix, normed, d_packed, d_outputs):
    d_wmix = jnp.dot(normed.T, d_packed, preferred_element_type=jnp.float32)
    d_normed = jnp.dot(d_packed, w_mix.T, preferred_element_type=jnp.float32)
    _, pull_back = jax.vjp(layer_norm, inputs.astype(jnp.float32), gain_vec)
    d_inputs, d_gain = pull_back(d_normed)
    return ((d_outputs.astype(jnp.float32) + d_inputs).astype(jnp.bfloat16), d_gain, d_wmix)

def block_backward(inputs, valid_rows, gain_vec, w_mix, w_out, saved_parts, d_outputs):
    normed, packed, mixed_rows = saved_parts
    d_wout = jnp.dot(mixed_rows.T, d_outputs, preferred_element_type=jnp.float32)
    d_mixed = jnp.dot(d_outputs, w_out.T, preferred_element_type=jnp.float32).astype(jnp.bfloat16)
    d_packed = attend_back(packed, valid_rows, d_mixed)
    d_inputs, d_gain, d_wmix = finish_back(inputs, gain_vec, w_mix, normed, d_packed, d_outputs)
    return (d_inputs, d_gain, d_wmix, d_wout)

def to_dilated(values_in, scenes, spacing):
    trailing = values_in.shape[1:]
    length = values_in.shape[0] // scenes
    shaped = values_in.reshape((scenes, length // spacing, spacing) + trailing)
    return jnp.swapaxes(shaped, 1, 2).reshape((scenes * length,) + trailing)

def from_dilated(values_in, scenes, spacing):
    trailing = values_in.shape[1:]
    length = values_in.shape[0] // scenes
    shaped = values_in.reshape((scenes, spacing, length // spacing) + trailing)
    return jnp.swapaxes(shaped, 1, 2).reshape((scenes * length,) + trailing)

def reference(x_in, counts, ln_gains, w_qkv, w_proj, cotangent):
    scenes = counts.shape[0]
    token_total = x_in.shape[0]
    length = token_total // scenes
    spacing = N_SEQ
    position = jnp.arange(length, dtype=jnp.int32)
    valid_near = (position[None, :] < counts[:, None]).astype(jnp.int32).reshape(token_total)
    valid_far = to_dilated(valid_near, scenes, spacing)
    first_out, first_saved = block_forward(x_in, valid_near, ln_gains[0], w_qkv[0], w_proj[0])
    second_in = to_dilated(first_out, scenes, spacing)
    second_far, second_saved = block_forward(second_in, valid_far, ln_gains[1], w_qkv[1], w_proj[1])
    second_out = from_dilated(second_far, scenes, spacing)
    keep_rows = (valid_near > 0)[:, None]
    result_out = jnp.where(keep_rows, second_out, jnp.zeros_like(second_out))
    d_result = jnp.where(keep_rows, cotangent, jnp.zeros_like(cotangent))
    d_second, gain_two, mix_two, proj_two = block_backward(second_in, valid_far, ln_gains[1], w_qkv[1], w_proj[1], second_saved, to_dilated(d_result, scenes, spacing))
    d_first = from_dilated(d_second, scenes, spacing)
    d_input, gain_one, mix_one, proj_one = block_backward(x_in, valid_near, ln_gains[0], w_qkv[0], w_proj[0], first_saved, d_first)
    factor = token_total ** (-0.5)
    return (result_out, d_input, jnp.stack([gain_one, gain_two]) * factor, jnp.stack([mix_one, mix_two]) * factor, jnp.stack([proj_one, proj_two]) * factor)
```

```python
import functools

import jax
import jax.numpy as jnp
from jax import lax
from jax.experimental import pallas as pl
from jax.experimental.pallas import tpu as pltpu
from jax.sharding import PartitionSpec as P

HEADS = 8
WIN = 1024
C = 256
HALF = 128
SPLIT = 8
PIECE = WIN // SPLIT
EPSILON = 1e-05
BLOCKED = -1e30
SCALE = (C // HEADS) ** (-0.5)
LOG2E = 1.4426950408889634
LN2 = 0.6931471805599453
f32 = jnp.float32
bf16 = jnp.bfloat16
NN = (((1,), (0,)), ((), ()))
NT = (((1,), (1,)), ((), ()))
TN = (((0,), (0,)), ((), ()))
dot = functools.partial(lax.dot_general, preferred_element_type=f32)
LIMIT = 56 * 2**20


def lanes():
    lane = lax.broadcasted_iota(jnp.int32, (1, HALF), 1)
    return lane >> 5, lane & 31


def norm_parts(x):
    average = jnp.mean(x, axis=-1, keepdims=True)
    centred = x - average
    spread = jnp.mean(centred * centred, axis=-1, keepdims=True)
    rstd = lax.rsqrt(spread + EPSILON)
    return centred * rstd, rstd


def project(normed, wq_ref, qkv_ref):
    packed = dot(normed, wq_ref[...], NN)
    for part in range(6):
        piece = packed[:, part * HALF : (part + 1) * HALF]
        if part < 2:
            piece = piece * (SCALE * LOG2E)
        qkv_ref[part] = piece.astype(bf16)


def group_extras(valid):
    _, l32 = lanes()
    vq = jnp.where(valid, 1.0, 0.0).astype(f32)
    for_q = jnp.where(l32 == 0, vq, jnp.where(l32 == 1, 1.0 - vq, 0.0)).astype(bf16)
    for_k = jnp.where(l32 == 0, BLOCKED * (1.0 - vq), jnp.where(l32 == 1, BLOCKED * vq, 0.0)).astype(bf16)
    return for_q, for_k


def head_masks(j):
    blk, _ = lanes()
    own = blk == j
    nxt = blk == ((j + 1) & 3)
    return own, nxt, own.astype(f32).astype(bf16), nxt.astype(f32).astype(bf16)


def attend_head(q, k, v, for_q, for_k, own_b, nxt_b):
    q_aug = q * own_b + for_q * nxt_b
    k_aug = k * (1 - nxt_b) + for_k * nxt_b
    scores = dot(q_aug, k_aug, NT)
    largest = jnp.max(scores, axis=1, keepdims=True)
    e = jnp.exp2(scores - largest).astype(bf16)
    return e, dot(e, v * own_b + (1 - own_b), NN)


def delta_parts(d_mixed, mixed, sums_next):
    blk_r = lax.broadcasted_iota(jnp.int32, (HALF, HALF), 0) >> 5
    blk_c = lax.broadcasted_iota(jnp.int32, (HALF, HALF), 1) >> 5
    shift = (blk_c == ((blk_r + 1) & 3)).astype(f32).astype(bf16)
    _, l32 = lanes()
    product = d_mixed * mixed
    high = product.astype(bf16)
    low = (product - high.astype(f32)).astype(bf16)
    delta = -(dot(high, shift, NN) + dot(low, shift, NN)) / sums_next
    high = delta.astype(bf16).astype(f32)
    extra = jnp.where(l32 == 0, high, jnp.where(l32 == 1, delta - high, 0.0)).astype(bf16)
    sums_own = pltpu.roll(sums_next, 96, 1)
    return (d_mixed / sums_own).astype(bf16), extra


def attend_back_head(e, q, k, v, d_own, extra, own_b, nxt_b):
    d_aug = d_own * own_b + extra * nxt_b
    d_weights = dot(d_aug, v * own_b + (1 - own_b), NT)
    d_scores = e * d_weights.astype(bf16)
    d_q = dot(d_scores, k, NN) * SCALE
    d_k = dot(d_scores, q, TN) * LN2
    d_v = dot(e, d_own, TN)
    return d_q, d_k, d_v


def block_finish(x, gain, wq_ref, dqkv_ref, dy, pay_ref):
    xhat, rstd = norm_parts(x)
    normed = (xhat * gain).astype(bf16)
    d_normed = jnp.zeros((WIN, C), f32)
    for part in range(6):
        cols = pl.ds(part * HALF, HALF)
        pay_ref[:, cols] = dot(normed, dqkv_ref[part], TN).astype(pay_ref.dtype)
        d_normed = d_normed + dot(dqkv_ref[part], wq_ref[:, cols], NT)
    d_gain = jnp.sum(d_normed * xhat, axis=0, keepdims=True)
    pay_ref[:, 1024:1152] = jnp.broadcast_to(d_gain, (HALF, C)).T.astype(pay_ref.dtype)
    d_hat = d_normed * gain
    mean_d = jnp.mean(d_hat, axis=-1, keepdims=True)
    mean_dx = jnp.mean(d_hat * xhat, axis=-1, keepdims=True)
    return dy.astype(f32) + rstd * (d_hat - mean_d - xhat * mean_dx)


def near_valid(n):
    i = lax.broadcasted_iota(jnp.int32, (WIN, 1), 0)
    return ((i & (PIECE - 1)) * SPLIT + (i >> 7)) < n


def split_kernel(n_ref, c_ref, o_ref, tmp):
    rows = lax.broadcasted_iota(jnp.int32, (WIN, 1), 0)
    kept = jnp.where(rows < n_ref[0], c_ref[...].astype(f32), 0.0)
    for g in range(2):
        tmp[g] = kept[:, g * HALF : (g + 1) * HALF]
    for g in range(2):
        for f in range(SPLIT):
            o_ref[f, :, g * HALF : (g + 1) * HALF] = tmp[g, pl.ds(f, PIECE, stride=SPLIT), :].astype(bf16)


def merge_kernel(r_ref, o_ref, tmp):
    for g in range(2):
        for f in range(SPLIT):
            tmp[g, pl.ds(f, PIECE, stride=SPLIT), :] = r_ref[f, :, g * HALF : (g + 1) * HALF].astype(f32)
    for g in range(2):
        o_ref[:, g * HALF : (g + 1) * HALF] = tmp[g].astype(bf16)


def near_forward_kernel(
    n_ref, x_ref, gain_ref, wq_ref, wo_ref, out_ref, xp_ref, qkv_ref, mixed_ref, sums_ref, e_ref, tmp, total, exq, exk
):
    step = pl.program_id(0)

    @pl.when(step == 0)
    def _():
        for g in range(2):
            tmp[g] = x_ref[:, g * HALF : (g + 1) * HALF].astype(f32)
        for g in range(2):
            for f in range(SPLIT):
                xp_ref[f * PIECE : (f + 1) * PIECE, g * HALF : (g + 1) * HALF] = tmp[
                    g, pl.ds(f, PIECE, stride=SPLIT), :
                ].astype(bf16)
        xhat, _ = norm_parts(xp_ref[...].astype(f32))
        project((xhat * gain_ref[...]).astype(bf16), wq_ref, qkv_ref)
        for_q, for_k = group_extras(near_valid(n_ref[0]))
        exq[...] = for_q
        exk[...] = for_k

    g = step >> 1
    for i in range(2):
        own, nxt, own_b, nxt_b = head_masks((step & 1) * 2 + i)
        e, both = attend_head(qkv_ref[g], qkv_ref[2 + g], qkv_ref[4 + g], exq[...], exk[...], own_b, nxt_b)
        e_ref[i] = e
        total[g] = jnp.where(own, both, total[g])
        sums_ref[g] = jnp.where(nxt, both, sums_ref[g])

    @pl.when(step == 3)
    def _():
        y = xp_ref[...].astype(f32)
        for g in range(2):
            mixed = (total[g] / pltpu.roll(sums_ref[g], 96, 1)).astype(bf16)
            mixed_ref[g] = mixed
            y = y + dot(mixed, wo_ref[g * HALF : (g + 1) * HALF, :], NN)
        out_ref[...] = y.astype(bf16)


def far_kernel(
    n_ref, x_ref, dy_ref, gain_ref, wq_ref, wo_ref, res_ref, dx_ref, pay_ref, qkv, dmix, mixed_s, dqkv, e_s, exq, exk
):
    g = pl.program_id(0)

    def valid():
        return lax.broadcasted_iota(jnp.int32, (WIN, 1), 0) < n_ref[0]

    @pl.when(g == 0)
    def _():
        xhat, _ = norm_parts(x_ref[...].astype(f32))
        project((xhat * gain_ref[...]).astype(bf16), wq_ref, qkv)
        for_q, for_k = group_extras(valid())
        exq[...] = for_q
        exk[...] = for_k
        d_mixed = dot(dy_ref[...], wo_ref[...], NT).astype(bf16)
        for i in range(2):
            dmix[i] = d_mixed[:, i * HALF : (i + 1) * HALF]

    q, k, v = qkv[g], qkv[2 + g], qkv[4 + g]
    total = sums = None
    for j in range(4):
        own, nxt, own_b, nxt_b = head_masks(j)
        e, both = attend_head(q, k, v, exq[...], exk[...], own_b, nxt_b)
        e_s[j] = e
        total = both if j == 0 else jnp.where(own, both, total)
        sums = both if j == 0 else jnp.where(nxt, both, sums)
    mixed = total / pltpu.roll(sums, 96, 1)
    mixed_s[g] = mixed.astype(bf16)
    d_own, extra = delta_parts(dmix[g].astype(f32), mixed, sums)
    dq = dk = dv = None
    for j in range(4):
        own, nxt, own_b, nxt_b = head_masks(j)
        one = attend_back_head(e_s[j], q, k, v, d_own, extra, own_b, nxt_b)
        dq, dk, dv = one if j == 0 else (jnp.where(own, a, b) for a, b in zip(one, (dq, dk, dv)))
    dqkv[g] = dq.astype(bf16)
    dqkv[2 + g] = dk.astype(bf16)
    dqkv[4 + g] = dv.astype(bf16)

    @pl.when(g == 1)
    def _():
        dy = dy_ref[...]
        x = x_ref[...].astype(f32)
        y = x
        for i in range(2):
            y = y + dot(mixed_s[i], wo_ref[i * HALF : (i + 1) * HALF, :], NN)
            pay_ref[i * HALF : (i + 1) * HALF, 768:1024] = dot(mixed_s[i], dy, TN).astype(pay_ref.dtype)
        res_ref[...] = jnp.where(valid(), y, 0.0).astype(bf16)
        dx_ref[...] = block_finish(x, gain_ref[...], wq_ref, dqkv, dy, pay_ref).astype(bf16)


def near_backward_kernel(
    dy_ref, xp_ref, gain_ref, wq_ref, wo_ref, qkv_ref, mixed_ref, sums_ref, e_ref, dx_ref, pay_ref, down, extra_s, dqkv, acc, tmp
):
    step = pl.program_id(0)

    @pl.when(step == 0)
    def _():
        dy = dy_ref[...]
        d_mixed = dot(dy, wo_ref[...], NT).astype(bf16).astype(f32)
        for i in range(2):
            d_own, extra = delta_parts(
                d_mixed[:, i * HALF : (i + 1) * HALF], mixed_ref[i].astype(f32), sums_ref[i]
            )
            down[i] = d_own
            extra_s[i] = extra
            pay_ref[i * HALF : (i + 1) * HALF, 768:1024] = dot(mixed_ref[i], dy, TN).astype(pay_ref.dtype)

    g = step >> 1
    q, k, v = qkv_ref[g], qkv_ref[2 + g], qkv_ref[4 + g]
    for i in range(2):
        own, nxt, own_b, nxt_b = head_masks((step & 1) * 2 + i)
        one = attend_back_head(e_ref[i], q, k, v, down[g], extra_s[g], own_b, nxt_b)
        for part in range(3):
            acc[part] = jnp.where(own, one[part], acc[part])

    @pl.when((step & 1) == 1)
    def _():
        for part in range(3):
            dqkv[2 * part + g] = acc[part].astype(bf16)

    @pl.when(step == 3)
    def _():
        dx = block_finish(xp_ref[...].astype(f32), gain_ref[...], wq_ref, dqkv, dy_ref[...], pay_ref)
        for g in range(2):
            for f in range(SPLIT):
                tmp[g, pl.ds(f, PIECE, stride=SPLIT), :] = dx[f * PIECE : (f + 1) * PIECE, g * HALF : (g + 1) * HALF]
        for g in range(2):
            dx_ref[:, g * HALF : (g + 1) * HALF] = tmp[g].astype(bf16)


def spec(shape):
    return pl.BlockSpec(shape, lambda i: (0,) * len(shape))


SCALAR = pl.BlockSpec(memory_space=pltpu.SMEM)
HEAD_PAIR = pl.BlockSpec((2, WIN, WIN), lambda i: (i, 0, 0))
PARAMS = pltpu.CompilerParams(vmem_limit_bytes=LIMIT)
ROWS = (WIN, C)
SPLIT_ROWS = (2, WIN, HALF)


def sds(shape, dtype):
    return jax.ShapeDtypeStruct(shape, dtype)


def cost(products):
    return pl.CostEstimate(flops=products * HEADS * 2 * WIN * WIN * HALF, bytes_accessed=2**24, transcendentals=2**23)


def split_rows(n, rows):
    return pl.pallas_call(
        split_kernel,
        in_specs=[SCALAR, pl.BlockSpec(memory_space=pltpu.VMEM)],
        out_specs=pl.BlockSpec(memory_space=pltpu.VMEM),
        out_shape=sds((SPLIT, PIECE, C), bf16),
        scratch_shapes=[pltpu.VMEM(SPLIT_ROWS, f32)],
        name="split_rows",
    )(n, rows)


def merge_rows(rows):
    return pl.pallas_call(
        merge_kernel,
        in_specs=[pl.BlockSpec(memory_space=pltpu.VMEM)],
        out_specs=pl.BlockSpec(memory_space=pltpu.VMEM),
        out_shape=sds(ROWS, bf16),
        scratch_shapes=[pltpu.VMEM(SPLIT_ROWS, f32)],
        name="merge_rows",
    )(rows)


def near_forward(n, x, gain, wq, wo):
    return pl.pallas_call(
        near_forward_kernel,
        grid=(4,),
        in_specs=[SCALAR, spec(ROWS), spec((1, C)), spec((C, 3 * C)), spec((C, C))],
        out_specs=[spec(ROWS), spec(ROWS), spec((6, WIN, HALF)), spec(SPLIT_ROWS), spec(SPLIT_ROWS), HEAD_PAIR],
        out_shape=[
            sds(ROWS, bf16),
            sds(ROWS, bf16),
            sds((6, WIN, HALF), bf16),
            sds(SPLIT_ROWS, bf16),
            sds(SPLIT_ROWS, f32),
            sds((HEADS, WIN, WIN), bf16),
        ],
        scratch_shapes=[
            pltpu.VMEM(SPLIT_ROWS, f32),
            pltpu.VMEM(SPLIT_ROWS, f32),
            pltpu.VMEM((WIN, HALF), bf16),
            pltpu.VMEM((WIN, HALF), bf16),
        ],
        compiler_params=PARAMS,
        cost_estimate=cost(2),
        name="near_forward",
    )(n, x, gain, wq, wo)


def far_both(n, x, dy, gain, wq, wo):
    return pl.pallas_call(
        far_kernel,
        grid=(2,),
        in_specs=[SCALAR, spec(ROWS), spec(ROWS), spec((1, C)), spec((C, 3 * C)), spec((C, C))],
        out_specs=[spec(ROWS), spec(ROWS), spec((C, 1152))],
        out_shape=[sds(ROWS, bf16), sds(ROWS, bf16), sds((C, 1152), bf16)],
        scratch_shapes=[
            pltpu.VMEM((6, WIN, HALF), bf16),
            pltpu.VMEM(SPLIT_ROWS, bf16),
            pltpu.VMEM(SPLIT_ROWS, bf16),
            pltpu.VMEM((6, WIN, HALF), bf16),
            pltpu.VMEM((4, WIN, WIN), bf16),
            pltpu.VMEM((WIN, HALF), bf16),
            pltpu.VMEM((WIN, HALF), bf16),
        ],
        compiler_params=PARAMS,
        cost_estimate=cost(6),
        name="far_both",
    )(n, x, dy, gain, wq, wo)


def near_backward(dy, xp, gain, wq, wo, qkv, mixed, sums, e):
    return pl.pallas_call(
        near_backward_kernel,
        grid=(4,),
        in_specs=[
            spec(ROWS),
            spec(ROWS),
            spec((1, C)),
            spec((C, 3 * C)),
            spec((C, C)),
            spec((6, WIN, HALF)),
            spec(SPLIT_ROWS),
            spec(SPLIT_ROWS),
            HEAD_PAIR,
        ],
        out_specs=[spec(ROWS), spec((C, 1152))],
        out_shape=[sds(ROWS, bf16), sds((C, 1152), bf16)],
        scratch_shapes=[
            pltpu.VMEM(SPLIT_ROWS, bf16),
            pltpu.VMEM(SPLIT_ROWS, bf16),
            pltpu.VMEM((6, WIN, HALF), bf16),
            pltpu.VMEM((3, WIN, HALF), f32),
            pltpu.VMEM(SPLIT_ROWS, f32),
        ],
        compiler_params=PARAMS,
        cost_estimate=cost(4),
        name="near_backward",
    )(dy, xp, gain, wq, wo, qkv, mixed, sums, e)


def exchange(rows, axis):
    return lax.all_to_all(rows, axis, split_axis=0, concat_axis=0, tiled=True)


def sum_everywhere(pay, factor):
    scenes, groups = lax.axis_size("scene"), lax.axis_size("seq")
    width = pay.shape[1]
    part = jnp.sum(exchange(pay.reshape(groups, scenes, width), "seq").astype(f32), axis=0)
    part = exchange(part.astype(bf16).reshape(scenes, 1, width), "scene").astype(f32)
    row = (jnp.sum(part, axis=0, keepdims=True) * factor).astype(bf16)
    rows = exchange(jnp.broadcast_to(row, (scenes, 1, width)), "scene").reshape(1, scenes, width)
    return exchange(jnp.broadcast_to(rows, (groups, scenes, width)), "seq").reshape(C, width)


def body(x_in, counts, ln_gains, w_qkv, w_proj, cotangent):
    groups = lax.axis_size("seq")
    place = lax.axis_index("seq")
    factor = (WIN * lax.axis_size("scene") * groups) ** (-0.5)
    n_near = counts - place * WIN
    n_far = (counts - place + groups - 1) // groups
    gain = ln_gains.reshape(2, 1, C)
    cot_far = exchange(split_rows(n_near, cotangent), "seq").reshape(ROWS)
    first, xp, qkv, mixed, sums, e = near_forward(n_near, x_in, gain[0], w_qkv[0], w_proj[0])
    first_far = exchange(first.reshape(SPLIT, PIECE, C), "seq").reshape(ROWS)
    result_far, d_first_far, pay_two = far_both(n_far, first_far, cot_far, gain[1], w_qkv[1], w_proj[1])
    d_first = exchange(d_first_far.reshape(SPLIT, PIECE, C), "seq").reshape(ROWS)
    result = merge_rows(exchange(result_far.reshape(SPLIT, PIECE, C), "seq"))
    two = sum_everywhere(pay_two, factor)
    d_input, pay_one = near_backward(d_first, xp, gain[0], w_qkv[0], w_proj[0], qkv, mixed, sums, e)
    one = sum_everywhere(pay_one, factor)
    both = jnp.stack([one, two]).astype(f32)
    return result, d_input, both[:, :, 1024], both[:, :, :768], both[:, :, 768:1024]


def solution(mesh):
    in_specs = (P(("scene", "seq"), None), P("scene"), P(), P(), P(), P(("scene", "seq"), None))
    out_specs = (P(("scene", "seq"), None), P(("scene", "seq"), None), P(), P(), P())
    return jax.shard_map(body, mesh=mesh, in_specs=in_specs, out_specs=out_specs, check_vma=False)
```

```python
import functools

import jax
import jax.numpy as jnp
from jax import lax
from jax.experimental import pallas as pl
from jax.experimental.pallas import tpu as pltpu
from jax.sharding import PartitionSpec as P

HEADS = 8
WIN = 1024
C = 256
HALF = 128
SPLIT = 8
PIECE = WIN // SPLIT
EPSILON = 1e-05
BLOCKED = -1e30
SCALE = (C // HEADS) ** (-0.5)
LOG2E = 1.4426950408889634
LN2 = 0.6931471805599453
f32 = jnp.float32
bf16 = jnp.bfloat16
NN = (((1,), (0,)), ((), ()))
NT = (((1,), (1,)), ((), ()))
TN = (((0,), (0,)), ((), ()))
dot = functools.partial(lax.dot_general, preferred_element_type=f32)
LIMIT = 56 * 2**20


def lanes():
    lane = lax.broadcasted_iota(jnp.int32, (1, HALF), 1)
    return lane >> 5, lane & 31


def norm_parts(x):
    average = jnp.mean(x, axis=-1, keepdims=True)
    centred = x - average
    spread = jnp.mean(centred * centred, axis=-1, keepdims=True)
    rstd = lax.rsqrt(spread + EPSILON)
    return centred * rstd, rstd


def project(normed, wq_ref, qkv_ref):
    packed = dot(normed, wq_ref[...], NN)
    for part in range(6):
        piece = packed[:, part * HALF : (part + 1) * HALF]
        if part < 2:
            piece = piece * (SCALE * LOG2E)
        qkv_ref[part] = piece.astype(bf16)


def group_extras(valid):
    _, l32 = lanes()
    vq = jnp.where(valid, 1.0, 0.0).astype(f32)
    for_q = jnp.where(l32 == 0, vq, jnp.where(l32 == 1, 1.0 - vq, 0.0)).astype(bf16)
    for_k = jnp.where(l32 == 0, BLOCKED * (1.0 - vq), jnp.where(l32 == 1, BLOCKED * vq, 0.0)).astype(bf16)
    return for_q, for_k


def head_masks(j):
    blk, _ = lanes()
    own = blk == j
    nxt = blk == ((j + 1) & 3)
    return own, nxt, own.astype(f32).astype(bf16), nxt.astype(f32).astype(bf16)


def attend_heads(heads, q, k, v, for_q, for_k, e_ref, vv_ref):
    for i, j in enumerate(heads):
        _, _, own_b, nxt_b = head_masks(j)
        q_aug = q * own_b + for_q * nxt_b
        k_aug = k * (1 - nxt_b) + for_k * nxt_b
        scores = dot(q_aug, k_aug, NT)
        largest = jnp.max(scores, axis=1, keepdims=True)
        e_ref[:, i * WIN : (i + 1) * WIN] = jnp.exp2(scores - largest).astype(bf16)
        vv_ref[i * WIN : (i + 1) * WIN, :HALF] = v * own_b
        vv_ref[i * WIN : (i + 1) * WIN, HALF:] = jnp.broadcast_to(own_b, (WIN, HALF))
    return dot(e_ref[...], vv_ref[...], NN)


def delta_parts(d_mixed, mixed, sums):
    blk_r = lax.broadcasted_iota(jnp.int32, (HALF, HALF), 0) >> 5
    blk_c = lax.broadcasted_iota(jnp.int32, (HALF, HALF), 1) >> 5
    same = (blk_c == blk_r).astype(f32).astype(bf16)
    _, l32 = lanes()
    product = d_mixed * mixed
    high = product.astype(bf16)
    low = (product - high.astype(f32)).astype(bf16)
    over = 1.0 / sums
    delta = pltpu.roll(-(dot(high, same, NN) + dot(low, same, NN)) * over, 32, 1)
    high = delta.astype(bf16).astype(f32)
    extra = jnp.where(l32 == 0, high, jnp.where(l32 == 1, delta - high, 0.0)).astype(bf16)
    return d_mixed * over, extra


def attend_back_heads(heads, e_ref, q_t, k, v, d_own, d_own_t, extra, ds_ref, kk_ref, dk_ref, dv_ref, base):
    for i, j in enumerate(heads):
        _, _, own_b, nxt_b = head_masks(j)
        e = e_ref[:, i * WIN : (i + 1) * WIN]
        d_weights = dot(d_own * own_b + extra * nxt_b, v * own_b + (1 - own_b), NT)
        d_scores = e * d_weights.astype(bf16)
        kk_ref[i * WIN : (i + 1) * WIN, :] = k * own_b
        rows = slice(i * 32, (i + 1) * 32)
        dst = pl.ds(pl.multiple_of(base + i * 32, 32), 32)
        dv_ref[dst, :] = dot(d_own_t[rows], e, NN).astype(bf16)
        ds_ref[:, i * WIN : (i + 1) * WIN] = d_scores
        dk_ref[dst, :] = (dot(q_t[rows], d_scores, NN) * LN2).astype(bf16)
    return dot(ds_ref[...], kk_ref[...], NN) * SCALE


def block_finish(x, gain, wq_ref, dq_ref, dk_ref, dv_ref, dy, put):
    xhat, rstd = norm_parts(x)
    normed = (xhat * gain).astype(bf16)
    d_normed = jnp.zeros((WIN, C), f32)
    for g in range(2):
        cols = slice(g * HALF, (g + 1) * HALF)
        put(g * HALF, dot(normed, dq_ref[g], TN))
        d_normed = d_normed + dot(dq_ref[g], wq_ref[:, cols], NT)
    for part, ref in ((1, dk_ref), (2, dv_ref)):
        put(part * C, dot(ref[...], normed, NN).T)
        w_t = wq_ref[:, part * C : (part + 1) * C].astype(f32).T.astype(bf16)
        d_normed = d_normed + dot(ref[...], w_t, TN)
    d_gain = jnp.sum(d_normed * xhat, axis=0, keepdims=True)
    d_hat = d_normed * gain
    mean_d = jnp.mean(d_hat, axis=-1, keepdims=True)
    mean_dx = jnp.mean(d_hat * xhat, axis=-1, keepdims=True)
    return dy.astype(f32) + rstd * (d_hat - mean_d - xhat * mean_dx), jnp.broadcast_to(d_gain, (HALF, C)).T


def near_valid(n):
    i = lax.broadcasted_iota(jnp.int32, (WIN, 1), 0)
    return ((i & (PIECE - 1)) * SPLIT + (i >> 7)) < n


def split_into(tmp, read, write):
    for g in range(2):
        tmp[g] = read(slice(g * HALF, (g + 1) * HALF))
    for g in range(2):
        for f in range(SPLIT):
            write(f, slice(g * HALF, (g + 1) * HALF), tmp[g, pl.ds(f, PIECE, stride=SPLIT), :].astype(bf16))


def merge_into(tmp, read, out_ref):
    for g in range(2):
        for f in range(SPLIT):
            tmp[g, pl.ds(f, PIECE, stride=SPLIT), :] = read(slice(f * PIECE, (f + 1) * PIECE), slice(g * HALF, (g + 1) * HALF))
    for g in range(2):
        out_ref[:, g * HALF : (g + 1) * HALF] = tmp[g].astype(bf16)


def near_forward_kernel(
    n_ref, x_ref, cot_ref, gain_ref, wq_ref, wo_ref, out_ref, xp_ref, qkv_ref, mixed_ref, sums_ref, e_ref, tmp, acc, vv, exq, exk
):
    step = pl.program_id(0)

    @pl.when(step == 0)
    def _():
        def put_x(f, cols, piece):
            xp_ref[f * PIECE : (f + 1) * PIECE, cols] = piece

        split_into(tmp, lambda cols: x_ref[:, cols].astype(f32), put_x)
        xhat, _ = norm_parts(xp_ref[...].astype(f32))
        project((xhat * gain_ref[0:1, :]).astype(bf16), wq_ref, qkv_ref)
        exq[...], exk[...] = group_extras(near_valid(n_ref[0]))

        def put_cot(f, cols, piece):
            out_ref[f * PIECE : (f + 1) * PIECE, C + cols.start : C + cols.stop] = piece

        kept = lax.broadcasted_iota(jnp.int32, (WIN, 1), 0) < n_ref[0]
        split_into(tmp, lambda cols: jnp.where(kept, cot_ref[:, cols].astype(f32), 0.0), put_cot)

    g = step >> 1
    first = (step & 1) * 2
    both = attend_heads(
        (first, first + 1), qkv_ref[g], qkv_ref[2 + g], qkv_ref[4 + g], exq[...], exk[...], e_ref, vv
    )

    @pl.when(first == 0)
    def _():
        acc[g] = both

    @pl.when(first != 0)
    def _():
        acc[g] = acc[g] + both

    @pl.when(step == 3)
    def _():
        y = xp_ref[...].astype(f32)
        for g in range(2):
            sums = acc[g, :, HALF:]
            sums_ref[g] = sums
            mixed = (acc[g, :, :HALF] / sums).astype(bf16)
            mixed_ref[g] = mixed
            y = y + dot(mixed, wo_ref[g * HALF : (g + 1) * HALF, :], NN)
        out_ref[:, :C] = y.astype(bf16)


def far_kernel(
    n_ref, in_ref, gain_ref, wq_ref, wo_ref, out_ref, pay_ref, qkv, dmix, mixed_s, dq, dk, dv, e_s, vv, kk, exq, exk
):
    g = pl.program_id(0)

    def valid():
        return lax.broadcasted_iota(jnp.int32, (WIN, 1), 0) < n_ref[0]

    @pl.when(g == 0)
    def _():
        xhat, _ = norm_parts(in_ref[:, :C].astype(f32))
        project((xhat * gain_ref[1:2, :]).astype(bf16), wq_ref, qkv)
        exq[...], exk[...] = group_extras(valid())
        d_mixed = dot(in_ref[:, C:], wo_ref[...], NT).astype(bf16)
        for i in range(2):
            dmix[i] = d_mixed[:, i * HALF : (i + 1) * HALF]

    q, k, v = qkv[g], qkv[2 + g], qkv[4 + g]
    both = attend_heads(range(4), q, k, v, exq[...], exk[...], e_s, vv)
    sums = both[:, HALF:]
    mixed = both[:, :HALF] / sums
    mixed_s[g] = mixed.astype(bf16)
    d_own, extra = delta_parts(dmix[g].astype(f32), mixed, sums)
    d_q = attend_back_heads(
        range(4), e_s, q.astype(f32).T.astype(bf16), k, v, d_own.astype(bf16), d_own.T.astype(bf16), extra, e_s, kk, dk, dv, g * HALF
    )
    dq[g] = d_q.astype(bf16)

    @pl.when(g == 1)
    def _():
        dy = in_ref[:, C:]
        x = in_ref[:, :C].astype(f32)
        y = x
        for i in range(2):
            y = y + dot(mixed_s[i], wo_ref[i * HALF : (i + 1) * HALF, :], NN)
            pay_ref[i * HALF : (i + 1) * HALF, 768:1024] = dot(mixed_s[i], dy, TN).astype(bf16)
        out_ref[:, C:] = jnp.where(valid(), y, 0.0).astype(bf16)

        def put(col, piece):
            pay_ref[:, col : col + piece.shape[1]] = piece.astype(bf16)

        dx, d_gain = block_finish(x, gain_ref[1:2, :], wq_ref, dq, dk, dv, dy, put)
        out_ref[:, :C] = dx.astype(bf16)
        put(1024, d_gain)


def near_backward_kernel(
    core_ref,
    in_ref,
    xp_ref,
    gain_ref,
    wq_ref,
    wo_ref,
    qkv_ref,
    mixed_ref,
    sums_ref,
    two_ref,
    e_ref,
    dx_ref,
    res_ref,
    keep_ref,
    send_ref,
    pay_ref,
    down,
    down_t,
    q_t,
    extra_s,
    dq,
    dk,
    dv,
    ds,
    kk,
    acc,
    tmp,
):
    step = pl.program_id(0)

    def put(col, piece):
        pay_ref[:, col : col + piece.shape[1]] = piece.astype(bf16)

    @pl.when(step == 0)
    def _():
        dy = in_ref[:, :C]
        d_mixed = dot(dy, wo_ref[...], NT).astype(bf16).astype(f32)
        for i in range(2):
            rows = slice(i * HALF, (i + 1) * HALF)
            d_own, extra = delta_parts(d_mixed[:, rows], mixed_ref[i].astype(f32), sums_ref[i])
            down[i] = d_own.astype(bf16)
            down_t[rows, :] = d_own.T.astype(bf16)
            q_t[rows, :] = qkv_ref[i].astype(f32).T.astype(bf16)
            extra_s[i] = extra
            pay_ref[rows, 768:1024] = dot(mixed_ref[i], dy, TN).astype(bf16)
        pay_ref[:, 1024:2048] = two_ref[:, :1024]
        merge_into(tmp, lambda rows, cols: in_ref[rows, C + cols.start : C + cols.stop].astype(f32), res_ref)

    g = step >> 1
    first = (step & 1) * 2
    base = pl.multiple_of(step * 64, 64)
    d_q = attend_back_heads(
        (first, first + 1),
        e_ref,
        q_t[pl.ds(base, 64), :],
        qkv_ref[2 + g],
        qkv_ref[4 + g],
        down[g],
        down_t[pl.ds(base, 64), :],
        extra_s[g],
        ds,
        kk,
        dk,
        dv,
        base,
    )

    @pl.when(first == 0)
    def _():
        acc[...] = d_q

    @pl.when(first != 0)
    def _():
        dq[g] = (acc[...] + d_q).astype(bf16)

    @pl.when(step == 3)
    def _():
        dx, d_gain = block_finish(
            xp_ref[...].astype(f32), gain_ref[0:1, :], wq_ref, dq, dk, dv, in_ref[:, :C], put
        )
        lane = lax.broadcasted_iota(jnp.int32, (1, HALF), 1)
        put(2048, jnp.where(lane == 0, d_gain, two_ref[:, 1024:1152].astype(f32)))
        merge_into(tmp, lambda rows, cols: dx[rows, cols], dx_ref)
        core = core_ref[0]
        keep_ref[...] = pay_ref[pl.ds(pl.multiple_of(core * HALF, HALF), HALF), :]
        send_ref[...] = pay_ref[pl.ds(pl.multiple_of((1 - core) * HALF, HALF), HALF), :]


def spread_kernel(core_ref, mine_ref, other_ref, gains_ref, qkv_ref, proj_ref, tmp):
    core = core_ref[0]
    for ref, half in ((mine_ref, core), (other_ref, 1 - core)):
        rows = pl.ds(pl.multiple_of(half * HALF, HALF), HALF)
        for b in range(2):
            qkv_ref[b, rows, :] = ref[:, b * 1024 : b * 1024 + 768].astype(f32)
            proj_ref[b, rows, :] = ref[:, b * 1024 + 768 : (b + 1) * 1024].astype(f32)
        tmp[rows, :] = ref[:, 2048:2176].astype(f32)
    gains_ref[...] = tmp[...].T[:2]


def layer(shape, which):
    return pl.BlockSpec((None,) + shape, lambda i: (which, 0, 0))


def spec(shape):
    return pl.BlockSpec(shape, lambda i: (0,) * len(shape))


SCALAR = pl.BlockSpec(memory_space=pltpu.SMEM)
HEAD_PAIR = pl.BlockSpec((WIN, 2 * WIN), lambda i: (0, i))
PARAMS = pltpu.CompilerParams(vmem_limit_bytes=LIMIT)
ROWS = (WIN, C)
PAIR_ROWS = (WIN, 2 * C)
SPLIT_ROWS = (2, WIN, HALF)


def sds(shape, dtype):
    return jax.ShapeDtypeStruct(shape, dtype)


def cost(products):
    return pl.CostEstimate(flops=products * HEADS * 2 * WIN * WIN * HALF, bytes_accessed=2**24, transcendentals=2**23)


def near_forward(n, x, cot, gain, wq, wo):
    return pl.pallas_call(
        near_forward_kernel,
        grid=(4,),
        in_specs=[SCALAR, spec(ROWS), spec(ROWS), spec((2, C)), layer((C, 3 * C), 0), layer((C, C), 0)],
        out_specs=[spec(PAIR_ROWS), spec(ROWS), spec((6, WIN, HALF)), spec(SPLIT_ROWS), spec(SPLIT_ROWS), HEAD_PAIR],
        out_shape=[
            sds(PAIR_ROWS, bf16),
            sds(ROWS, bf16),
            sds((6, WIN, HALF), bf16),
            sds(SPLIT_ROWS, bf16),
            sds(SPLIT_ROWS, f32),
            sds((WIN, HEADS * WIN), bf16),
        ],
        scratch_shapes=[
            pltpu.VMEM(SPLIT_ROWS, f32),
            pltpu.VMEM((2, WIN, C), f32),
            pltpu.VMEM((2 * WIN, C), bf16),
            pltpu.VMEM((WIN, HALF), bf16),
            pltpu.VMEM((WIN, HALF), bf16),
        ],
        compiler_params=PARAMS,
        cost_estimate=cost(2),
        name="near_forward",
    )(n, x, cot, gain, wq, wo)


def far_both(n, rows, gain, wq, wo):
    return pl.pallas_call(
        far_kernel,
        grid=(2,),
        in_specs=[SCALAR, spec(PAIR_ROWS), spec((2, C)), layer((C, 3 * C), 1), layer((C, C), 1)],
        out_specs=[spec(PAIR_ROWS), spec((C, 1152))],
        out_shape=[sds(PAIR_ROWS, bf16), sds((C, 1152), bf16)],
        scratch_shapes=[
            pltpu.VMEM((6, WIN, HALF), bf16),
            pltpu.VMEM(SPLIT_ROWS, bf16),
            pltpu.VMEM(SPLIT_ROWS, bf16),
            pltpu.VMEM(SPLIT_ROWS, bf16),
            pltpu.VMEM((C, WIN), bf16),
            pltpu.VMEM((C, WIN), bf16),
            pltpu.VMEM((WIN, 4 * WIN), bf16),
            pltpu.VMEM((4 * WIN, C), bf16),
            pltpu.VMEM((4 * WIN, HALF), bf16),
            pltpu.VMEM((WIN, HALF), bf16),
            pltpu.VMEM((WIN, HALF), bf16),
        ],
        compiler_params=PARAMS,
        cost_estimate=cost(6),
        name="far_both",
    )(n, rows, gain, wq, wo)


def near_backward(core, rows, xp, gain, wq, wo, qkv, mixed, sums, two, e):
    return pl.pallas_call(
        near_backward_kernel,
        grid=(4,),
        in_specs=[
            SCALAR,
            spec(PAIR_ROWS),
            spec(ROWS),
            spec((2, C)),
            layer((C, 3 * C), 0),
            layer((C, C), 0),
            spec((6, WIN, HALF)),
            spec(SPLIT_ROWS),
            spec(SPLIT_ROWS),
            spec((C, 1152)),
            HEAD_PAIR,
        ],
        out_specs=[spec(ROWS), spec(ROWS), spec((HALF, 2176)), spec((HALF, 2176))],
        out_shape=[sds(ROWS, bf16), sds(ROWS, bf16), sds((HALF, 2176), bf16), sds((HALF, 2176), bf16)],
        scratch_shapes=[
            pltpu.VMEM((C, 2176), bf16),
            pltpu.VMEM(SPLIT_ROWS, bf16),
            pltpu.VMEM((C, WIN), bf16),
            pltpu.VMEM((C, WIN), bf16),
            pltpu.VMEM(SPLIT_ROWS, bf16),
            pltpu.VMEM(SPLIT_ROWS, bf16),
            pltpu.VMEM((C, WIN), bf16),
            pltpu.VMEM((C, WIN), bf16),
            pltpu.VMEM((WIN, 2 * WIN), bf16),
            pltpu.VMEM((2 * WIN, HALF), bf16),
            pltpu.VMEM((WIN, HALF), f32),
            pltpu.VMEM(SPLIT_ROWS, f32),
        ],
        compiler_params=PARAMS,
        cost_estimate=cost(4),
        name="near_backward",
    )(core, rows, xp, gain, wq, wo, qkv, mixed, sums, two, e)


def spread(core, mine, other):
    vmem = pl.BlockSpec(memory_space=pltpu.VMEM)
    return pl.pallas_call(
        spread_kernel,
        in_specs=[SCALAR, vmem, vmem],
        out_shape=[sds((2, C), f32), sds((2, C, 3 * C), f32), sds((2, C, C), f32)],
        scratch_shapes=[pltpu.VMEM((C, HALF), f32)],
        compiler_params=PARAMS,
        name="spread",
    )(core, mine, other)


def exchange(rows, axis, groups=None):
    return lax.all_to_all(rows, axis, split_axis=0, concat_axis=0, tiled=True, axis_index_groups=groups)


def sum_everywhere(keep, send, factor):
    scenes, groups = lax.axis_size("scene"), lax.axis_size("seq")
    width = keep.shape[1]
    pair = [(i, i ^ 1) for i in range(groups)]
    chips = [list(range(core, groups, 2)) for core in range(2)]
    many = groups // 2
    part = (keep.astype(f32) + lax.ppermute(send, "seq", pair).astype(f32)).astype(bf16)
    part = jnp.sum(exchange(part.reshape(many, scenes, width), "seq", chips).astype(f32), axis=0)
    part = exchange(part.astype(bf16).reshape(scenes, 1, width), "scene").astype(f32)
    row = (jnp.sum(part, axis=0, keepdims=True) * factor).astype(bf16)
    rows = exchange(jnp.broadcast_to(row, (scenes, 1, width)), "scene").reshape(1, scenes, width)
    mine = exchange(jnp.broadcast_to(rows, (many, scenes, width)), "seq", chips).reshape(HALF, width)
    return mine, lax.ppermute(mine, "seq", pair)


def body(x_in, counts, ln_gains, w_qkv, w_proj, cotangent):
    groups = lax.axis_size("seq")
    place = lax.axis_index("seq")
    factor = (WIN * lax.axis_size("scene") * groups) ** (-0.5)
    n_near = counts - place * WIN
    n_far = (counts - place + groups - 1) // groups

    def swap(rows):
        return exchange(rows.reshape(SPLIT, PIECE, 2 * C), "seq").reshape(PAIR_ROWS)

    first, xp, qkv, mixed, sums, e = near_forward(n_near, x_in, cotangent, ln_gains, w_qkv, w_proj)
    back, pay_two = far_both(n_far, swap(first), ln_gains, w_qkv, w_proj)
    core = jnp.full((1,), place % 2, jnp.int32)
    d_input, result, keep, send = near_backward(
        core, swap(back), xp, ln_gains, w_qkv, w_proj, qkv, mixed, sums, pay_two, e
    )
    gains, grads, projs = spread(core, *sum_everywhere(keep, send, factor))
    return result, d_input, gains, grads, projs


def solution(mesh):
    in_specs = (P(("scene", "seq"), None), P("scene"), P(), P(), P(), P(("scene", "seq"), None))
    out_specs = (P(("scene", "seq"), None), P(("scene", "seq"), None), P(), P(), P())
    return jax.shard_map(body, mesh=mesh, in_specs=in_specs, out_specs=out_specs, check_vma=False)
```

```python
import functools

import jax
import jax.numpy as jnp
from jax import lax
from jax.experimental import pallas as pl
from jax.experimental.pallas import tpu as pltpu
from jax.sharding import PartitionSpec as P

HEADS = 8
WIN = 1024
C = 256
HALF = 128
SPLIT = 8
PIECE = WIN // SPLIT
EPSILON = 1e-05
BLOCKED = -1e30
SCALE = (C // HEADS) ** (-0.5)
LOG2E = 1.4426950408889634
LN2 = 0.6931471805599453
f32 = jnp.float32
bf16 = jnp.bfloat16
NN = (((1,), (0,)), ((), ()))
NT = (((1,), (1,)), ((), ()))
TN = (((0,), (0,)), ((), ()))
dot = functools.partial(lax.dot_general, preferred_element_type=f32)
LIMIT = 56 * 2**20


def lanes():
    lane = lax.broadcasted_iota(jnp.int32, (1, HALF), 1)
    return lane >> 5, lane & 31


def norm_parts(x):
    average = jnp.mean(x, axis=-1, keepdims=True)
    centred = x - average
    spread = jnp.mean(centred * centred, axis=-1, keepdims=True)
    rstd = lax.rsqrt(spread + EPSILON)
    return centred * rstd, rstd


def project(normed, wq_ref, qkv_ref):
    packed = dot(normed, wq_ref[...], NN)
    for part in range(6):
        piece = packed[:, part * HALF : (part + 1) * HALF]
        if part < 2:
            piece = piece * (SCALE * LOG2E)
        qkv_ref[part] = piece.astype(bf16)


def group_extras(valid):
    _, l32 = lanes()
    vq = jnp.where(valid, 1.0, 0.0).astype(f32)
    for_q = jnp.where(l32 == 0, vq, jnp.where(l32 == 1, 1.0 - vq, 0.0)).astype(bf16)
    for_k = jnp.where(l32 == 0, BLOCKED * (1.0 - vq), jnp.where(l32 == 1, BLOCKED * vq, 0.0)).astype(bf16)
    return for_q, for_k


def head_masks(j):
    blk, _ = lanes()
    own = blk == j
    nxt = blk == ((j + 1) & 3)
    return own, nxt, own.astype(f32).astype(bf16), nxt.astype(f32).astype(bf16)


def attend_heads(heads, q, k, v, for_q, for_k, e_ref):
    total = sums = 0.0
    for i, j in enumerate(heads):
        own, nxt, own_b, nxt_b = head_masks(j)
        q_aug = q * own_b + for_q * nxt_b
        k_aug = k * (1 - nxt_b) + for_k * nxt_b
        scores = dot(q_aug, k_aug, NT)
        largest = jnp.max(scores, axis=1, keepdims=True)
        e = jnp.exp2(scores - largest).astype(bf16)
        e_ref[:, i * WIN : (i + 1) * WIN] = e
        both = dot(e, v * own_b + (1 - own_b), NN)
        total = total + jnp.where(own, both, 0.0)
        sums = sums + jnp.where(nxt, both, 0.0)
    return total, pltpu.roll(sums, 96, 1)


def delta_parts(d_mixed, mixed, sums):
    blk_r = lax.broadcasted_iota(jnp.int32, (HALF, HALF), 0) >> 5
    blk_c = lax.broadcasted_iota(jnp.int32, (HALF, HALF), 1) >> 5
    same = (blk_c == blk_r).astype(f32).astype(bf16)
    _, l32 = lanes()
    product = d_mixed * mixed
    high = product.astype(bf16)
    low = (product - high.astype(f32)).astype(bf16)
    over = 1.0 / sums
    delta = pltpu.roll(-(dot(high, same, NN) + dot(low, same, NN)) * over, 32, 1)
    high = delta.astype(bf16).astype(f32)
    extra = jnp.where(l32 == 0, high, jnp.where(l32 == 1, delta - high, 0.0)).astype(bf16)
    return d_mixed * over, extra


def attend_back_heads(heads, e_ref, q_t, k, v, d_own, d_own_t, extra, dk_ref, dv_ref, base):
    d_q = 0.0
    for i, j in enumerate(heads):
        _, _, own_b, nxt_b = head_masks(j)
        e = e_ref[:, i * WIN : (i + 1) * WIN]
        d_weights = dot(d_own * own_b + extra * nxt_b, v * own_b + (1 - own_b), NT)
        d_scores = e * d_weights.astype(bf16)
        rows = slice(i * 32, (i + 1) * 32)
        dst = pl.ds(pl.multiple_of(base + i * 32, 32), 32)
        dv_ref[dst, :] = dot(d_own_t[rows], e, NN).astype(bf16)
        dk_ref[dst, :] = (dot(q_t[rows], d_scores, NN) * LN2).astype(bf16)
        d_q = d_q + dot(d_scores, k * own_b, NN)
    return d_q * SCALE


def weight_grads(normed, dq_ref, dk_ref, dv_ref, put):
    for g in range(2):
        put(g * HALF, dot(normed, dq_ref[g], TN))
    put(C, dot(dk_ref[...], normed, NN).T)
    put(2 * C, dot(dv_ref[...], normed, NN).T)


def input_grad(x, gain, wq_ref, dq_ref, dk_ref, dv_ref, dy):
    xhat, rstd = norm_parts(x)
    d_normed = jnp.zeros((WIN, C), f32)
    for g in range(2):
        d_normed = d_normed + dot(dq_ref[g], wq_ref[:, g * HALF : (g + 1) * HALF], NT)
    for part, ref in ((1, dk_ref), (2, dv_ref)):
        w_t = wq_ref[:, part * C : (part + 1) * C].astype(f32).T.astype(bf16)
        d_normed = d_normed + dot(ref[...], w_t, TN)
    d_hat = d_normed * gain
    mean_d = jnp.mean(d_hat, axis=-1, keepdims=True)
    mean_dx = jnp.mean(d_hat * xhat, axis=-1, keepdims=True)
    return dy.astype(f32) + rstd * (d_hat - mean_d - xhat * mean_dx)


def near_valid(n):
    i = lax.broadcasted_iota(jnp.int32, (WIN, 1), 0)
    return ((i & (PIECE - 1)) * SPLIT + (i >> 7)) < n


def split_into(tmp, read, write):
    for g in range(2):
        tmp[g] = read(slice(g * HALF, (g + 1) * HALF))
    for g in range(2):
        for f in range(SPLIT):
            write(f, slice(g * HALF, (g + 1) * HALF), tmp[g, pl.ds(f, PIECE, stride=SPLIT), :].astype(bf16))


def merge_into(tmp, read, out_ref):
    for g in range(2):
        for f in range(SPLIT):
            tmp[g, pl.ds(f, PIECE, stride=SPLIT), :] = read(slice(f * PIECE, (f + 1) * PIECE), slice(g * HALF, (g + 1) * HALF))
    for g in range(2):
        out_ref[:, g * HALF : (g + 1) * HALF] = tmp[g].astype(bf16)


def near_forward_kernel(
    n_ref, x_ref, cot_ref, gain_ref, wq_ref, wo_ref, out_ref, xp_ref, normed_ref, qkv_ref, mixed_ref, sums_ref, e_ref, tmp, acc, exq, exk
):
    step = pl.program_id(0)

    @pl.when(step == 0)
    def _():
        def put_x(f, cols, piece):
            xp_ref[f * PIECE : (f + 1) * PIECE, cols] = piece

        split_into(tmp, lambda cols: x_ref[:, cols].astype(f32), put_x)
        xhat, _ = norm_parts(xp_ref[...].astype(f32))
        normed_ref[...] = (xhat * gain_ref[0:1, :]).astype(bf16)
        project(normed_ref[...], wq_ref, qkv_ref)
        exq[...], exk[...] = group_extras(near_valid(n_ref[0]))

        def put_cot(f, cols, piece):
            out_ref[f * PIECE : (f + 1) * PIECE, C + cols.start : C + cols.stop] = piece

        kept = lax.broadcasted_iota(jnp.int32, (WIN, 1), 0) < n_ref[0]
        split_into(tmp, lambda cols: jnp.where(kept, cot_ref[:, cols].astype(f32), 0.0), put_cot)

    g = step >> 1
    first = (step & 1) * 2
    total, sums = attend_heads(
        (first, first + 1), qkv_ref[g], qkv_ref[2 + g], qkv_ref[4 + g], exq[...], exk[...], e_ref
    )

    @pl.when(first == 0)
    def _():
        acc[g, :, :HALF] = total
        acc[g, :, HALF:] = sums

    @pl.when(first != 0)
    def _():
        acc[g, :, :HALF] = acc[g, :, :HALF] + total
        acc[g, :, HALF:] = acc[g, :, HALF:] + sums

    @pl.when(step == 3)
    def _():
        y = xp_ref[...].astype(f32)
        for g in range(2):
            sums = acc[g, :, HALF:]
            sums_ref[g] = sums
            mixed = (acc[g, :, :HALF] / sums).astype(bf16)
            mixed_ref[g] = mixed
            y = y + dot(mixed, wo_ref[g * HALF : (g + 1) * HALF, :], NN)
        out_ref[:, :C] = y.astype(bf16)


def far_kernel(
    n_ref, in_ref, gain_ref, wq_ref, wo_ref, out_ref, mixed_s, dq, dk, dv, qkv, dmix, e_s, exq, exk
):
    g = pl.program_id(0)

    def valid():
        return lax.broadcasted_iota(jnp.int32, (WIN, 1), 0) < n_ref[0]

    @pl.when(g == 0)
    def _():
        xhat, _ = norm_parts(in_ref[:, :C].astype(f32))
        project((xhat * gain_ref[1:2, :]).astype(bf16), wq_ref, qkv)
        exq[...], exk[...] = group_extras(valid())
        d_mixed = dot(in_ref[:, C:], wo_ref[...], NT).astype(bf16)
        for i in range(2):
            dmix[i] = d_mixed[:, i * HALF : (i + 1) * HALF]

    q, k, v = qkv[g], qkv[2 + g], qkv[4 + g]
    total, sums = attend_heads(range(4), q, k, v, exq[...], exk[...], e_s)
    mixed = total / sums
    mixed_s[g] = mixed.astype(bf16)
    d_own, extra = delta_parts(dmix[g].astype(f32), mixed, sums)
    d_q = attend_back_heads(
        range(4), e_s, q.astype(f32).T.astype(bf16), k, v, d_own.astype(bf16), d_own.T.astype(bf16), extra, dk, dv, g * HALF
    )
    dq[g] = d_q.astype(bf16)

    @pl.when(g == 1)
    def _():
        x = in_ref[:, :C].astype(f32)
        y = x
        for i in range(2):
            y = y + dot(mixed_s[i], wo_ref[i * HALF : (i + 1) * HALF, :], NN)
        out_ref[:, C:] = jnp.where(valid(), y, 0.0).astype(bf16)
        out_ref[:, :C] = input_grad(x, gain_ref[1:2, :], wq_ref, dq, dk, dv, in_ref[:, C:]).astype(bf16)


def far_grads_kernel(in_ref, gain_ref, mixed_ref, dq, dk, dv, pay_ref):
    def put(col, piece):
        pay_ref[:, col : col + piece.shape[1]] = piece.astype(bf16)

    for i in range(2):
        pay_ref[i * HALF : (i + 1) * HALF, 768:1024] = dot(mixed_ref[i], in_ref[:, C:], TN).astype(bf16)
    xhat, _ = norm_parts(in_ref[:, :C].astype(f32))
    weight_grads((xhat * gain_ref[1:2, :]).astype(bf16), dq, dk, dv, put)


def near_finish_kernel(in_ref, xp_ref, gain_ref, wq_ref, dq, dk, dv, dx_ref, res_ref, tmp):
    merge_into(tmp, lambda rows, cols: in_ref[rows, C + cols.start : C + cols.stop].astype(f32), res_ref)
    dx = input_grad(xp_ref[...].astype(f32), gain_ref[0:1, :], wq_ref, dq, dk, dv, in_ref[:, :C])
    merge_into(tmp, lambda rows, cols: dx[rows, cols], dx_ref)


def near_backward_kernel(
    core_ref,
    in_ref,
    normed_ref,
    wo_ref,
    qkv_ref,
    mixed_ref,
    sums_ref,
    two_ref,
    e_ref,
    keep_ref,
    send_ref,
    dq,
    dk,
    dv,
    pay_ref,
    down,
    down_t,
    q_t,
    extra_s,
    acc,
    e_s,
    sem,
):
    step = pl.program_id(0)

    def put(col, piece):
        pay_ref[:, col : col + piece.shape[1]] = piece.astype(bf16)

    def fetch(i):
        slot = i & 1
        cols = pl.ds(pl.multiple_of(i * 2 * WIN, 2 * WIN), 2 * WIN)
        return pltpu.make_async_copy(e_ref.at[:, cols], e_s.at[slot], sem.at[slot])

    @pl.when(step == 0)
    def _():
        fetch(0).start()
        fetch(1).start()
        dy = in_ref[:, :C]
        d_mixed = dot(dy, wo_ref[...], NT).astype(bf16).astype(f32)
        for i in range(2):
            rows = slice(i * HALF, (i + 1) * HALF)
            d_own, extra = delta_parts(d_mixed[:, rows], mixed_ref[i].astype(f32), sums_ref[i])
            down[i] = d_own.astype(bf16)
            down_t[rows, :] = d_own.T.astype(bf16)
            q_t[rows, :] = qkv_ref[i].astype(f32).T.astype(bf16)
            extra_s[i] = extra
            pay_ref[rows, 768:1024] = dot(mixed_ref[i], dy, TN).astype(bf16)
        pay_ref[:, 1024:2048] = two_ref[...]

    fetch(step).wait()
    g = step >> 1
    first = (step & 1) * 2
    base = pl.multiple_of(step * 64, 64)
    d_q = attend_back_heads(
        (first, first + 1),
        e_s.at[step & 1],
        q_t[pl.ds(base, 64), :],
        qkv_ref[2 + g],
        qkv_ref[4 + g],
        down[g],
        down_t[pl.ds(base, 64), :],
        extra_s[g],
        dk,
        dv,
        base,
    )

    @pl.when(step < 2)
    def _():
        fetch(step + 2).start()

    @pl.when(first == 0)
    def _():
        acc[...] = d_q

    @pl.when(first != 0)
    def _():
        dq[g] = (acc[...] + d_q).astype(bf16)

    @pl.when(step == 3)
    def _():
        weight_grads(normed_ref[...], dq, dk, dv, put)
        core = core_ref[0]
        keep_ref[...] = pay_ref[pl.ds(pl.multiple_of(core * HALF, HALF), HALF), :]
        send_ref[...] = pay_ref[pl.ds(pl.multiple_of((1 - core) * HALF, HALF), HALF), :]


def spread_kernel(core_ref, mine_ref, other_ref, gain_ref, wq_ref, gains_ref, qkv_ref, proj_ref):
    core = core_ref[0]
    for ref, half in ((mine_ref, core), (other_ref, 1 - core)):
        rows = pl.ds(pl.multiple_of(half * HALF, HALF), HALF)
        for b in range(2):
            qkv_ref[b, rows, :] = ref[:, b * 1024 : b * 1024 + 768].astype(f32)
            proj_ref[b, rows, :] = ref[:, b * 1024 + 768 : (b + 1) * 1024].astype(f32)
    for b in range(2):
        along = jnp.sum(qkv_ref[b] * wq_ref[b].astype(f32), axis=1, keepdims=True)
        gains_ref[b : b + 1, :] = jnp.broadcast_to(along, (C, HALF)).T[:1] / gain_ref[b : b + 1, :]


def layer(shape, which):
    return pl.BlockSpec((None,) + shape, lambda i: (which, 0, 0))


def spec(shape):
    return pl.BlockSpec(shape, lambda i: (0,) * len(shape))


SCALAR = pl.BlockSpec(memory_space=pltpu.SMEM)
HEAD_PAIR = pl.BlockSpec((WIN, 2 * WIN), lambda i: (0, i))
PARAMS = pltpu.CompilerParams(vmem_limit_bytes=LIMIT)
ROWS = (WIN, C)
PAIR_ROWS = (WIN, 2 * C)
SPLIT_ROWS = (2, WIN, HALF)


def sds(shape, dtype):
    return jax.ShapeDtypeStruct(shape, dtype)


def cost(products):
    return pl.CostEstimate(flops=products * HEADS * 2 * WIN * WIN * HALF, bytes_accessed=2**24, transcendentals=2**23)


def near_forward(n, x, cot, gain, wq, wo):
    return pl.pallas_call(
        near_forward_kernel,
        grid=(4,),
        in_specs=[SCALAR, spec(ROWS), spec(ROWS), spec((2, C)), layer((C, 3 * C), 0), layer((C, C), 0)],
        out_specs=[spec(PAIR_ROWS), spec(ROWS), spec(ROWS), spec((6, WIN, HALF)), spec(SPLIT_ROWS), spec(SPLIT_ROWS), HEAD_PAIR],
        out_shape=[
            sds(PAIR_ROWS, bf16),
            sds(ROWS, bf16),
            sds(ROWS, bf16),
            sds((6, WIN, HALF), bf16),
            sds(SPLIT_ROWS, bf16),
            sds(SPLIT_ROWS, f32),
            sds((WIN, HEADS * WIN), bf16),
        ],
        scratch_shapes=[
            pltpu.VMEM(SPLIT_ROWS, f32),
            pltpu.VMEM((2, WIN, C), f32),
            pltpu.VMEM((WIN, HALF), bf16),
            pltpu.VMEM((WIN, HALF), bf16),
        ],
        compiler_params=PARAMS,
        cost_estimate=cost(2),
        name="near_forward",
    )(n, x, cot, gain, wq, wo)


D_ROWS = [SPLIT_ROWS, (C, WIN), (C, WIN)]
D_SHAPES = [sds(shape, bf16) for shape in D_ROWS]
D_SPECS = [spec(shape) for shape in D_ROWS]


def far_both(n, rows, gain, wq, wo):
    return pl.pallas_call(
        far_kernel,
        grid=(2,),
        in_specs=[SCALAR, spec(PAIR_ROWS), spec((2, C)), layer((C, 3 * C), 1), layer((C, C), 1)],
        out_specs=[spec(PAIR_ROWS), spec(SPLIT_ROWS), *D_SPECS],
        out_shape=[sds(PAIR_ROWS, bf16), sds(SPLIT_ROWS, bf16), *D_SHAPES],
        scratch_shapes=[
            pltpu.VMEM((6, WIN, HALF), bf16),
            pltpu.VMEM(SPLIT_ROWS, bf16),
            pltpu.VMEM((WIN, 4 * WIN), bf16),
            pltpu.VMEM((WIN, HALF), bf16),
            pltpu.VMEM((WIN, HALF), bf16),
        ],
        compiler_params=PARAMS,
        cost_estimate=cost(6),
        name="far_both",
    )(n, rows, gain, wq, wo)


def far_grads(rows, gain, mixed, dq, dk, dv):
    return pl.pallas_call(
        far_grads_kernel,
        grid=(1,),
        in_specs=[spec(PAIR_ROWS), spec((2, C)), spec(SPLIT_ROWS), *D_SPECS],
        out_specs=spec((C, 1024)),
        out_shape=sds((C, 1024), bf16),
        compiler_params=PARAMS,
        cost_estimate=pl.CostEstimate(flops=2**30, bytes_accessed=2**22, transcendentals=0),
        name="far_grads",
    )(rows, gain, mixed, dq, dk, dv)


def near_finish(rows, xp, gain, wq, dq, dk, dv):
    return pl.pallas_call(
        near_finish_kernel,
        grid=(1,),
        in_specs=[spec(PAIR_ROWS), spec(ROWS), spec((2, C)), layer((C, 3 * C), 0), *D_SPECS],
        out_specs=[spec(ROWS), spec(ROWS)],
        out_shape=[sds(ROWS, bf16), sds(ROWS, bf16)],
        scratch_shapes=[pltpu.VMEM(SPLIT_ROWS, f32)],
        compiler_params=PARAMS,
        cost_estimate=pl.CostEstimate(flops=2**30, bytes_accessed=2**22, transcendentals=0),
        name="near_finish",
    )(rows, xp, gain, wq, dq, dk, dv)


def near_backward(core, rows, normed, wo, qkv, mixed, sums, two, e):
    return pl.pallas_call(
        near_backward_kernel,
        grid=(4,),
        in_specs=[
            SCALAR,
            spec(PAIR_ROWS),
            spec(ROWS),
            layer((C, C), 0),
            spec((6, WIN, HALF)),
            spec(SPLIT_ROWS),
            spec(SPLIT_ROWS),
            spec((C, 1024)),
            pl.BlockSpec(memory_space=pl.ANY),
        ],
        out_specs=[spec((HALF, 2048)), spec((HALF, 2048)), *D_SPECS],
        out_shape=[sds((HALF, 2048), bf16), sds((HALF, 2048), bf16), *D_SHAPES],
        scratch_shapes=[
            pltpu.VMEM((C, 2048), bf16),
            pltpu.VMEM(SPLIT_ROWS, bf16),
            pltpu.VMEM((C, WIN), bf16),
            pltpu.VMEM((C, WIN), bf16),
            pltpu.VMEM(SPLIT_ROWS, bf16),
            pltpu.VMEM((WIN, HALF), f32),
            pltpu.VMEM((2, WIN, 2 * WIN), bf16),
            pltpu.SemaphoreType.DMA((2,)),
        ],
        compiler_params=PARAMS,
        cost_estimate=cost(4),
        name="near_backward",
    )(core, rows, normed, wo, qkv, mixed, sums, two, e)


def spread(core, mine, other, gain, wq):
    vmem = pl.BlockSpec(memory_space=pltpu.VMEM)
    return pl.pallas_call(
        spread_kernel,
        in_specs=[SCALAR, vmem, vmem, vmem, vmem],
        out_shape=[sds((2, C), f32), sds((2, C, 3 * C), f32), sds((2, C, C), f32)],
        compiler_params=PARAMS,
        name="spread",
    )(core, mine, other, gain, wq)


def exchange(rows, axis, groups=None):
    return lax.all_to_all(rows, axis, split_axis=0, concat_axis=0, tiled=True, axis_index_groups=groups)


def sum_everywhere(keep, send, factor, beside):
    scenes, groups = lax.axis_size("scene"), lax.axis_size("seq")
    width = keep.shape[1]
    pair = [(i, i ^ 1) for i in range(groups)]
    chips = [list(range(core, groups, 2)) for core in range(2)]
    many = groups // 2
    part = (keep.astype(f32) + lax.ppermute(send, "seq", pair).astype(f32)).astype(bf16)
    part = exchange(part.reshape(many, scenes, width), "seq", chips)
    part, beside = lax.optimization_barrier((part, beside))
    part = jnp.sum(part.astype(f32), axis=0)
    part = exchange(part.astype(bf16).reshape(scenes, 1, width), "scene").astype(f32)
    row = (jnp.sum(part, axis=0, keepdims=True) * factor).astype(bf16)
    rows = exchange(jnp.broadcast_to(row, (scenes, 1, width)), "scene").reshape(1, scenes, width)
    mine = exchange(jnp.broadcast_to(rows, (many, scenes, width)), "seq", chips).reshape(HALF, width)
    return mine, lax.ppermute(mine, "seq", pair), beside


def body(x_in, counts, ln_gains, w_qkv, w_proj, cotangent):
    groups = lax.axis_size("seq")
    place = lax.axis_index("seq")
    factor = (WIN * lax.axis_size("scene") * groups) ** (-0.5)
    n_near = counts - place * WIN
    n_far = (counts - place + groups - 1) // groups

    def swap(rows):
        return exchange(rows.reshape(SPLIT, PIECE, 2 * C), "seq").reshape(PAIR_ROWS)

    core = jnp.full((1,), place % 2, jnp.int32)
    first, xp, normed, qkv, mixed, sums, e = near_forward(n_near, x_in, cotangent, ln_gains, w_qkv, w_proj)
    rows_far = swap(first)
    back, *far_parts = far_both(n_far, rows_far, ln_gains, w_qkv, w_proj)
    rows = swap(back)
    two = far_grads(rows_far, ln_gains, *far_parts)
    keep, send, *d_rows = near_backward(core, rows, normed, w_proj, qkv, mixed, sums, two, e)
    beside = near_finish(rows, xp, ln_gains, w_qkv, *d_rows)
    mine, other, (d_input, result) = sum_everywhere(keep, send, factor, tuple(beside))
    gains, grads, projs = spread(core, mine, other, ln_gains, w_qkv)
    return result, d_input, gains, grads, projs


def solution(mesh):
    in_specs = (P(("scene", "seq"), None), P("scene"), P(), P(), P(), P(("scene", "seq"), None))
    out_specs = (P(("scene", "seq"), None), P(("scene", "seq"), None), P(), P(), P())
    return jax.shard_map(body, mesh=mesh, in_specs=in_specs, out_specs=out_specs, check_vma=False)
```

```python
import functools

import jax
import jax.numpy as jnp
from jax import lax
from jax.experimental import pallas as pl
from jax.experimental.pallas import tpu as pltpu
from jax.sharding import PartitionSpec as P

HEADS = 8
WIN = 1024
C = 256
HALF = 128
SPLIT = 8
PIECE = WIN // SPLIT
EPSILON = 1e-05
BLOCKED = -1e30
SCALE = (C // HEADS) ** (-0.5)
LOG2E = 1.4426950408889634
LN2 = 0.6931471805599453
f32 = jnp.float32
bf16 = jnp.bfloat16
NN = (((1,), (0,)), ((), ()))
NT = (((1,), (1,)), ((), ()))
TN = (((0,), (0,)), ((), ()))
dot = functools.partial(lax.dot_general, preferred_element_type=f32)
LIMIT = 56 * 2**20


def lanes():
    lane = lax.broadcasted_iota(jnp.int32, (1, HALF), 1)
    return lane >> 5, lane & 31


def norm_parts(x):
    average = jnp.mean(x, axis=-1, keepdims=True)
    centred = x - average
    spread = jnp.mean(centred * centred, axis=-1, keepdims=True)
    rstd = lax.rsqrt(spread + EPSILON)
    return centred * rstd, rstd


def project(normed, wq_ref, qkv_ref):
    packed = dot(normed, wq_ref[...], NN)
    for part in range(6):
        piece = packed[:, part * HALF : (part + 1) * HALF]
        if part < 2:
            piece = piece * (SCALE * LOG2E)
        qkv_ref[part] = piece.astype(bf16)


def group_extras(valid):
    _, l32 = lanes()
    vq = jnp.where(valid, 1.0, 0.0).astype(f32)
    for_q = jnp.where(l32 == 0, vq, jnp.where(l32 == 1, 1.0 - vq, 0.0)).astype(bf16)
    for_k = jnp.where(l32 == 0, BLOCKED * (1.0 - vq), jnp.where(l32 == 1, BLOCKED * vq, 0.0)).astype(bf16)
    return for_q, for_k


def head_masks(j):
    blk, _ = lanes()
    own = blk == j
    nxt = blk == ((j + 1) & 3)
    return own, nxt, own.astype(f32).astype(bf16), nxt.astype(f32).astype(bf16)


def attend_heads(heads, q, k, v, for_q, for_k, e_ref):
    total = sums = 0.0
    for i, j in enumerate(heads):
        own, nxt, own_b, nxt_b = head_masks(j)
        q_aug = q * own_b + for_q * nxt_b
        k_aug = k * (1 - nxt_b) + for_k * nxt_b
        scores = dot(q_aug, k_aug, NT)
        largest = jnp.max(scores, axis=1, keepdims=True)
        e = jnp.exp2(scores - largest).astype(bf16)
        e_ref[:, i * WIN : (i + 1) * WIN] = e
        both = dot(e, v * own_b + (1 - own_b), NN)
        total = total + jnp.where(own, both, 0.0)
        sums = sums + jnp.where(nxt, both, 0.0)
    return total, pltpu.roll(sums, 96, 1)


def delta_parts(d_mixed, mixed, sums):
    blk_r = lax.broadcasted_iota(jnp.int32, (HALF, HALF), 0) >> 5
    blk_c = lax.broadcasted_iota(jnp.int32, (HALF, HALF), 1) >> 5
    same = (blk_c == blk_r).astype(f32).astype(bf16)
    _, l32 = lanes()
    product = d_mixed * mixed
    high = product.astype(bf16)
    low = (product - high.astype(f32)).astype(bf16)
    over = 1.0 / sums
    delta = pltpu.roll(-(dot(high, same, NN) + dot(low, same, NN)) * over, 32, 1)
    high = delta.astype(bf16).astype(f32)
    extra = jnp.where(l32 == 0, high, jnp.where(l32 == 1, delta - high, 0.0)).astype(bf16)
    return d_mixed * over, extra


def attend_back_heads(heads, e_ref, q_t, k, v, d_own, d_own_t, extra, dk_ref, dv_ref, base):
    d_q = 0.0
    for i, j in enumerate(heads):
        _, _, own_b, nxt_b = head_masks(j)
        e = e_ref[:, i * WIN : (i + 1) * WIN]
        d_weights = dot(d_own * own_b + extra * nxt_b, v * own_b + (1 - own_b), NT)
        d_scores = e * d_weights.astype(bf16)
        rows = slice(i * 32, (i + 1) * 32)
        dst = pl.ds(pl.multiple_of(base + i * 32, 32), 32)
        dv_ref[dst, :] = dot(d_own_t[rows], e, NN).astype(bf16)
        dk_ref[dst, :] = (dot(q_t[rows], d_scores, NN) * LN2).astype(bf16)
        d_q = d_q + dot(d_scores, k * own_b, NN)
    return d_q * SCALE


def weight_grads(normed, dq_ref, dk_ref, dv_ref, put):
    for g in range(2):
        put(g * HALF, dot(normed, dq_ref[g], TN))
    put(C, dot(dk_ref[...], normed, NN).T)
    put(2 * C, dot(dv_ref[...], normed, NN).T)


def input_grad(x, gain, wq_ref, dq_ref, dk_ref, dv_ref, dy):
    xhat, rstd = norm_parts(x)
    d_normed = jnp.zeros((WIN, C), f32)
    for g in range(2):
        d_normed = d_normed + dot(dq_ref[g], wq_ref[:, g * HALF : (g + 1) * HALF], NT)
    for part, ref in ((1, dk_ref), (2, dv_ref)):
        w_t = wq_ref[:, part * C : (part + 1) * C].astype(f32).T.astype(bf16)
        d_normed = d_normed + dot(ref[...], w_t, TN)
    d_hat = d_normed * gain
    mean_d = jnp.mean(d_hat, axis=-1, keepdims=True)
    mean_dx = jnp.mean(d_hat * xhat, axis=-1, keepdims=True)
    return dy.astype(f32) + rstd * (d_hat - mean_d - xhat * mean_dx)


def near_valid(n):
    i = lax.broadcasted_iota(jnp.int32, (WIN, 1), 0)
    return ((i & (PIECE - 1)) * SPLIT + (i >> 7)) < n


def split_into(tmp, read, write):
    for g in range(2):
        tmp[g] = read(slice(g * HALF, (g + 1) * HALF))
    for g in range(2):
        for f in range(SPLIT):
            write(f, slice(g * HALF, (g + 1) * HALF), tmp[g, pl.ds(f, PIECE, stride=SPLIT), :].astype(bf16))


def merge_into(tmp, read, out_ref):
    for g in range(2):
        for f in range(SPLIT):
            tmp[g, pl.ds(f, PIECE, stride=SPLIT), :] = read(slice(f * PIECE, (f + 1) * PIECE), slice(g * HALF, (g + 1) * HALF))
    for g in range(2):
        out_ref[:, g * HALF : (g + 1) * HALF] = tmp[g].astype(bf16)


def near_forward_kernel(
    n_ref, x_ref, cot_ref, gain_ref, wq_ref, wo_ref, out_ref, xp_out, normed_out, qkv_out, mixed_ref, sums_ref, e_out, tmp, acc, exq, exk, xp_ref, normed_ref, qkv_ref, e_s, sem
):
    step = pl.program_id(0)
    early = [
        pltpu.make_async_copy(src, dst, sem.at[2 + i])
        for i, (src, dst) in enumerate(((xp_ref, xp_out), (normed_ref, normed_out), (qkv_ref, qkv_out)))
    ]

    def save(i):
        slot = i & 1
        cols = pl.ds(pl.multiple_of(i * 2 * WIN, 2 * WIN), 2 * WIN)
        return pltpu.make_async_copy(e_s.at[slot], e_out.at[:, cols], sem.at[slot])

    @pl.when(step == 0)
    def _():
        def put_x(f, cols, piece):
            xp_ref[f * PIECE : (f + 1) * PIECE, cols] = piece

        split_into(tmp, lambda cols: x_ref[:, cols].astype(f32), put_x)
        xhat, _ = norm_parts(xp_ref[...].astype(f32))
        normed_ref[...] = (xhat * gain_ref[0:1, :]).astype(bf16)
        project(normed_ref[...], wq_ref, qkv_ref)
        for copy in early:
            copy.start()
        exq[...], exk[...] = group_extras(near_valid(n_ref[0]))

        def put_cot(f, cols, piece):
            out_ref[f * PIECE : (f + 1) * PIECE, C + cols.start : C + cols.stop] = piece

        kept = lax.broadcasted_iota(jnp.int32, (WIN, 1), 0) < n_ref[0]
        split_into(tmp, lambda cols: jnp.where(kept, cot_ref[:, cols].astype(f32), 0.0), put_cot)

    @pl.when(step >= 2)
    def _():
        save(step - 2).wait()

    g = step >> 1
    first = (step & 1) * 2
    total, sums = attend_heads(
        (first, first + 1), qkv_ref[g], qkv_ref[2 + g], qkv_ref[4 + g], exq[...], exk[...], e_s.at[step & 1]
    )
    save(step).start()

    @pl.when(first == 0)
    def _():
        acc[g, :, :HALF] = total
        acc[g, :, HALF:] = sums

    @pl.when(first != 0)
    def _():
        acc[g, :, :HALF] = acc[g, :, :HALF] + total
        acc[g, :, HALF:] = acc[g, :, HALF:] + sums

    @pl.when(step == 3)
    def _():
        y = xp_ref[...].astype(f32)
        for g in range(2):
            sums = acc[g, :, HALF:]
            sums_ref[g] = sums
            mixed = (acc[g, :, :HALF] / sums).astype(bf16)
            mixed_ref[g] = mixed
            y = y + dot(mixed, wo_ref[g * HALF : (g + 1) * HALF, :], NN)
        out_ref[:, :C] = y.astype(bf16)
        for copy in early:
            copy.wait()
        save(2).wait()
        save(3).wait()


def far_kernel(
    n_ref, in_ref, gain_ref, wq_ref, wo_ref, out_ref, mixed_s, dq, dk, dv, qkv, dmix, e_s, exq, exk
):
    g = pl.program_id(0)

    def valid():
        return lax.broadcasted_iota(jnp.int32, (WIN, 1), 0) < n_ref[0]

    @pl.when(g == 0)
    def _():
        xhat, _ = norm_parts(in_ref[:, :C].astype(f32))
        project((xhat * gain_ref[1:2, :]).astype(bf16), wq_ref, qkv)
        exq[...], exk[...] = group_extras(valid())
        d_mixed = dot(in_ref[:, C:], wo_ref[...], NT).astype(bf16)
        for i in range(2):
            dmix[i] = d_mixed[:, i * HALF : (i + 1) * HALF]

    q, k, v = qkv[g], qkv[2 + g], qkv[4 + g]
    total, sums = attend_heads(range(4), q, k, v, exq[...], exk[...], e_s)
    mixed = total / sums
    mixed_s[g] = mixed.astype(bf16)
    d_own, extra = delta_parts(dmix[g].astype(f32), mixed, sums)
    d_q = attend_back_heads(
        range(4), e_s, q.astype(f32).T.astype(bf16), k, v, d_own.astype(bf16), d_own.T.astype(bf16), extra, dk, dv, g * HALF
    )
    dq[g] = d_q.astype(bf16)

    @pl.when(g == 1)
    def _():
        x = in_ref[:, :C].astype(f32)
        y = x
        for i in range(2):
            y = y + dot(mixed_s[i], wo_ref[i * HALF : (i + 1) * HALF, :], NN)
        out_ref[:, C:] = jnp.where(valid(), y, 0.0).astype(bf16)
        out_ref[:, :C] = input_grad(x, gain_ref[1:2, :], wq_ref, dq, dk, dv, in_ref[:, C:]).astype(bf16)


def far_grads_kernel(in_ref, gain_ref, mixed_ref, dq, dk, dv, pay_ref):
    def put(col, piece):
        pay_ref[:, col : col + piece.shape[1]] = piece.astype(bf16)

    for i in range(2):
        pay_ref[i * HALF : (i + 1) * HALF, 768:1024] = dot(mixed_ref[i], in_ref[:, C:], TN).astype(bf16)
    xhat, _ = norm_parts(in_ref[:, :C].astype(f32))
    weight_grads((xhat * gain_ref[1:2, :]).astype(bf16), dq, dk, dv, put)


def near_finish_kernel(in_ref, xp_ref, gain_ref, wq_ref, dq, dk, dv, dx_ref, res_ref, tmp):
    merge_into(tmp, lambda rows, cols: in_ref[rows, C + cols.start : C + cols.stop].astype(f32), res_ref)
    dx = input_grad(xp_ref[...].astype(f32), gain_ref[0:1, :], wq_ref, dq, dk, dv, in_ref[:, :C])
    merge_into(tmp, lambda rows, cols: dx[rows, cols], dx_ref)


def near_backward_kernel(
    core_ref,
    in_ref,
    normed_ref,
    wo_ref,
    qkv_ref,
    mixed_ref,
    sums_ref,
    two_ref,
    e_ref,
    keep_ref,
    send_ref,
    dq,
    dk,
    dv,
    pay_ref,
    down,
    down_t,
    q_t,
    extra_s,
    e_s,
    sem,
):
    step = pl.program_id(0)

    def put(col, piece):
        pay_ref[:, col : col + piece.shape[1]] = piece.astype(bf16)

    def fetch(i):
        cols = pl.ds(pl.multiple_of(i * 4 * WIN, 4 * WIN), 4 * WIN)
        return pltpu.make_async_copy(e_ref.at[:, cols], e_s.at[i], sem.at[i])

    @pl.when(step == 0)
    def _():
        fetch(0).start()
        fetch(1).start()
        dy = in_ref[:, :C]
        d_mixed = dot(dy, wo_ref[...], NT).astype(bf16).astype(f32)
        for i in range(2):
            rows = slice(i * HALF, (i + 1) * HALF)
            d_own, extra = delta_parts(d_mixed[:, rows], mixed_ref[i].astype(f32), sums_ref[i])
            down[i] = d_own.astype(bf16)
            down_t[rows, :] = d_own.T.astype(bf16)
            q_t[rows, :] = qkv_ref[i].astype(f32).T.astype(bf16)
            extra_s[i] = extra
            pay_ref[rows, 768:1024] = dot(mixed_ref[i], dy, TN).astype(bf16)
        pay_ref[:, 1024:2048] = two_ref[...]

    fetch(step).wait()
    g = step
    base = pl.multiple_of(step * HALF, HALF)
    d_q = attend_back_heads(
        range(4),
        e_s.at[step],
        q_t[pl.ds(base, HALF), :],
        qkv_ref[2 + g],
        qkv_ref[4 + g],
        down[g],
        down_t[pl.ds(base, HALF), :],
        extra_s[g],
        dk,
        dv,
        base,
    )

    dq[g] = d_q.astype(bf16)

    @pl.when(step == 1)
    def _():
        weight_grads(normed_ref[...], dq, dk, dv, put)
        core = core_ref[0]
        keep_ref[...] = pay_ref[pl.ds(pl.multiple_of(core * HALF, HALF), HALF), :]
        send_ref[...] = pay_ref[pl.ds(pl.multiple_of((1 - core) * HALF, HALF), HALF), :]


def spread_kernel(core_ref, mine_ref, other_ref, gain_ref, wq_ref, gains_ref, qkv_ref, proj_ref):
    core = core_ref[0]
    for ref, half in ((mine_ref, core), (other_ref, 1 - core)):
        rows = pl.ds(pl.multiple_of(half * HALF, HALF), HALF)
        for b in range(2):
            qkv_ref[b, rows, :] = ref[:, b * 1024 : b * 1024 + 768].astype(f32)
            proj_ref[b, rows, :] = ref[:, b * 1024 + 768 : (b + 1) * 1024].astype(f32)
    for b in range(2):
        along = jnp.sum(qkv_ref[b] * wq_ref[b].astype(f32), axis=1, keepdims=True)
        gains_ref[b : b + 1, :] = jnp.broadcast_to(along, (C, HALF)).T[:1] / gain_ref[b : b + 1, :]


def layer(shape, which):
    return pl.BlockSpec((None,) + shape, lambda i: (which, 0, 0))


def spec(shape):
    return pl.BlockSpec(shape, lambda i: (0,) * len(shape))


SCALAR = pl.BlockSpec(memory_space=pltpu.SMEM)
ANY = pl.BlockSpec(memory_space=pl.ANY)
PARAMS = pltpu.CompilerParams(vmem_limit_bytes=LIMIT)
ROWS = (WIN, C)
PAIR_ROWS = (WIN, 2 * C)
SPLIT_ROWS = (2, WIN, HALF)


def sds(shape, dtype):
    return jax.ShapeDtypeStruct(shape, dtype)


def cost(products):
    return pl.CostEstimate(flops=products * HEADS * 2 * WIN * WIN * HALF, bytes_accessed=2**24, transcendentals=2**23)


def near_forward(n, x, cot, gain, wq, wo):
    return pl.pallas_call(
        near_forward_kernel,
        grid=(4,),
        in_specs=[SCALAR, spec(ROWS), spec(ROWS), spec((2, C)), layer((C, 3 * C), 0), layer((C, C), 0)],
        out_specs=[spec(PAIR_ROWS), ANY, ANY, ANY, spec(SPLIT_ROWS), spec(SPLIT_ROWS), ANY],
        out_shape=[
            sds(PAIR_ROWS, bf16),
            sds(ROWS, bf16),
            sds(ROWS, bf16),
            sds((6, WIN, HALF), bf16),
            sds(SPLIT_ROWS, bf16),
            sds(SPLIT_ROWS, f32),
            sds((WIN, HEADS * WIN), bf16),
        ],
        scratch_shapes=[
            pltpu.VMEM(SPLIT_ROWS, f32),
            pltpu.VMEM((2, WIN, C), f32),
            pltpu.VMEM((WIN, HALF), bf16),
            pltpu.VMEM((WIN, HALF), bf16),
            pltpu.VMEM(ROWS, bf16),
            pltpu.VMEM(ROWS, bf16),
            pltpu.VMEM((6, WIN, HALF), bf16),
            pltpu.VMEM((2, WIN, 2 * WIN), bf16),
            pltpu.SemaphoreType.DMA((5,)),
        ],
        compiler_params=PARAMS,
        cost_estimate=cost(2),
        name="near_forward",
    )(n, x, cot, gain, wq, wo)


D_ROWS = [SPLIT_ROWS, (C, WIN), (C, WIN)]
D_SHAPES = [sds(shape, bf16) for shape in D_ROWS]
D_SPECS = [spec(shape) for shape in D_ROWS]


def far_both(n, rows, gain, wq, wo):
    return pl.pallas_call(
        far_kernel,
        grid=(2,),
        in_specs=[SCALAR, spec(PAIR_ROWS), spec((2, C)), layer((C, 3 * C), 1), layer((C, C), 1)],
        out_specs=[spec(PAIR_ROWS), spec(SPLIT_ROWS), *D_SPECS],
        out_shape=[sds(PAIR_ROWS, bf16), sds(SPLIT_ROWS, bf16), *D_SHAPES],
        scratch_shapes=[
            pltpu.VMEM((6, WIN, HALF), bf16),
            pltpu.VMEM(SPLIT_ROWS, bf16),
            pltpu.VMEM((WIN, 4 * WIN), bf16),
            pltpu.VMEM((WIN, HALF), bf16),
            pltpu.VMEM((WIN, HALF), bf16),
        ],
        compiler_params=PARAMS,
        cost_estimate=cost(6),
        name="far_both",
    )(n, rows, gain, wq, wo)


def far_grads(rows, gain, mixed, dq, dk, dv):
    return pl.pallas_call(
        far_grads_kernel,
        grid=(1,),
        in_specs=[spec(PAIR_ROWS), spec((2, C)), spec(SPLIT_ROWS), *D_SPECS],
        out_specs=spec((C, 1024)),
        out_shape=sds((C, 1024), bf16),
        compiler_params=PARAMS,
        cost_estimate=pl.CostEstimate(flops=2**30, bytes_accessed=2**22, transcendentals=0),
        name="far_grads",
    )(rows, gain, mixed, dq, dk, dv)


def near_finish(rows, xp, gain, wq, dq, dk, dv):
    return pl.pallas_call(
        near_finish_kernel,
        grid=(1,),
        in_specs=[spec(PAIR_ROWS), spec(ROWS), spec((2, C)), layer((C, 3 * C), 0), *D_SPECS],
        out_specs=[spec(ROWS), spec(ROWS)],
        out_shape=[sds(ROWS, bf16), sds(ROWS, bf16)],
        scratch_shapes=[pltpu.VMEM(SPLIT_ROWS, f32)],
        compiler_params=PARAMS,
        cost_estimate=pl.CostEstimate(flops=2**30, bytes_accessed=2**22, transcendentals=0),
        name="near_finish",
    )(rows, xp, gain, wq, dq, dk, dv)


def near_backward(core, rows, normed, wo, qkv, mixed, sums, two, e):
    return pl.pallas_call(
        near_backward_kernel,
        grid=(2,),
        in_specs=[
            SCALAR,
            spec(PAIR_ROWS),
            spec(ROWS),
            layer((C, C), 0),
            spec((6, WIN, HALF)),
            spec(SPLIT_ROWS),
            spec(SPLIT_ROWS),
            spec((C, 1024)),
            pl.BlockSpec(memory_space=pl.ANY),
        ],
        out_specs=[spec((HALF, 2048)), spec((HALF, 2048)), *D_SPECS],
        out_shape=[sds((HALF, 2048), bf16), sds((HALF, 2048), bf16), *D_SHAPES],
        scratch_shapes=[
            pltpu.VMEM((C, 2048), bf16),
            pltpu.VMEM(SPLIT_ROWS, bf16),
            pltpu.VMEM((C, WIN), bf16),
            pltpu.VMEM((C, WIN), bf16),
            pltpu.VMEM(SPLIT_ROWS, bf16),
            pltpu.VMEM((2, WIN, 4 * WIN), bf16),
            pltpu.SemaphoreType.DMA((2,)),
        ],
        compiler_params=PARAMS,
        cost_estimate=cost(4),
        name="near_backward",
    )(core, rows, normed, wo, qkv, mixed, sums, two, e)


def spread(core, mine, other, gain, wq):
    vmem = pl.BlockSpec(memory_space=pltpu.VMEM)
    return pl.pallas_call(
        spread_kernel,
        in_specs=[SCALAR, vmem, vmem, vmem, vmem],
        out_shape=[sds((2, C), f32), sds((2, C, 3 * C), f32), sds((2, C, C), f32)],
        compiler_params=PARAMS,
        name="spread",
    )(core, mine, other, gain, wq)


def exchange(rows, axis, groups=None):
    return lax.all_to_all(rows, axis, split_axis=0, concat_axis=0, tiled=True, axis_index_groups=groups)


def sum_everywhere(keep, send, factor, beside):
    scenes, groups = lax.axis_size("scene"), lax.axis_size("seq")
    width = keep.shape[1]
    pair = [(i, i ^ 1) for i in range(groups)]
    chips = [list(range(core, groups, 2)) for core in range(2)]
    many = groups // 2
    part = (keep.astype(f32) + lax.ppermute(send, "seq", pair).astype(f32)).astype(bf16)
    part = exchange(part.reshape(many, scenes, width), "seq", chips)
    part, beside = lax.optimization_barrier((part, beside))
    part = jnp.sum(part.astype(f32), axis=0)
    part = exchange(part.astype(bf16).reshape(scenes, 1, width), "scene").astype(f32)
    row = (jnp.sum(part, axis=0, keepdims=True) * factor).astype(bf16)
    rows = exchange(jnp.broadcast_to(row, (scenes, 1, width)), "scene").reshape(1, scenes, width)
    mine = exchange(jnp.broadcast_to(rows, (many, scenes, width)), "seq", chips).reshape(HALF, width)
    return mine, lax.ppermute(mine, "seq", pair), beside


def body(x_in, counts, ln_gains, w_qkv, w_proj, cotangent):
    groups = lax.axis_size("seq")
    place = lax.axis_index("seq")
    factor = (WIN * lax.axis_size("scene") * groups) ** (-0.5)
    n_near = counts - place * WIN
    n_far = (counts - place + groups - 1) // groups

    def swap(rows):
        return exchange(rows.reshape(SPLIT, PIECE, 2 * C), "seq").reshape(PAIR_ROWS)

    core = jnp.full((1,), place % 2, jnp.int32)
    first, xp, normed, qkv, mixed, sums, e = near_forward(n_near, x_in, cotangent, ln_gains, w_qkv, w_proj)
    rows_far = swap(first)
    back, *far_parts = far_both(n_far, rows_far, ln_gains, w_qkv, w_proj)
    rows = swap(back)
    two = far_grads(rows_far, ln_gains, *far_parts)
    keep, send, *d_rows = near_backward(core, rows, normed, w_proj, qkv, mixed, sums, two, e)
    beside = near_finish(rows, xp, ln_gains, w_qkv, *d_rows)
    mine, other, (d_input, result) = sum_everywhere(keep, send, factor, tuple(beside))
    gains, grads, projs = spread(core, mine, other, ln_gains, w_qkv)
    return result, d_input, gains, grads, projs


def solution(mesh):
    in_specs = (P(("scene", "seq"), None), P("scene"), P(), P(), P(), P(("scene", "seq"), None))
    out_specs = (P(("scene", "seq"), None), P(("scene", "seq"), None), P(), P(), P())
    return jax.shard_map(body, mesh=mesh, in_specs=in_specs, out_specs=out_specs, check_vma=False)
```

```python
import functools

import jax
import jax.numpy as jnp
from jax import lax
from jax.experimental import pallas as pl
from jax.experimental.pallas import tpu as pltpu
from jax.sharding import PartitionSpec as P

HEADS = 8
WIN = 1024
C = 256
HALF = 128
SPLIT = 8
PIECE = WIN // SPLIT
EPSILON = 1e-05
BLOCKED = -1e30
SCALE = (C // HEADS) ** (-0.5)
LOG2E = 1.4426950408889634
LN2 = 0.6931471805599453
f32 = jnp.float32
bf16 = jnp.bfloat16
NN = (((1,), (0,)), ((), ()))
NT = (((1,), (1,)), ((), ()))
TN = (((0,), (0,)), ((), ()))
dot = functools.partial(lax.dot_general, preferred_element_type=f32)
LIMIT = 56 * 2**20


def lanes():
    lane = lax.broadcasted_iota(jnp.int32, (1, HALF), 1)
    return lane >> 5, lane & 31


def norm_parts(x):
    average = jnp.mean(x, axis=-1, keepdims=True)
    centred = x - average
    spread = jnp.mean(centred * centred, axis=-1, keepdims=True)
    rstd = lax.rsqrt(spread + EPSILON)
    return centred * rstd, rstd


def project(normed, wq_ref, qkv_ref):
    packed = dot(normed, wq_ref[...], NN)
    for part in range(6):
        piece = packed[:, part * HALF : (part + 1) * HALF]
        if part < 2:
            piece = piece * (SCALE * LOG2E)
        qkv_ref[part] = piece.astype(bf16)


def group_extras(valid):
    _, l32 = lanes()
    vq = jnp.where(valid, 1.0, 0.0).astype(f32)
    for_q = jnp.where(l32 == 0, vq, jnp.where(l32 == 1, 1.0 - vq, 0.0)).astype(bf16)
    for_k = jnp.where(l32 == 0, BLOCKED * (1.0 - vq), jnp.where(l32 == 1, BLOCKED * vq, 0.0)).astype(bf16)
    return for_q, for_k


def head_masks(j):
    blk, _ = lanes()
    own = blk == j
    nxt = blk == ((j + 1) & 3)
    return own, nxt, own.astype(f32).astype(bf16), nxt.astype(f32).astype(bf16)


def attend_heads(heads, q, k, v, for_q, for_k, e_ref):
    total = sums = 0.0
    for i, j in enumerate(heads):
        own, nxt, own_b, nxt_b = head_masks(j)
        q_aug = q * own_b + for_q * nxt_b
        k_aug = k * (1 - nxt_b) + for_k * nxt_b
        scores = dot(q_aug, k_aug, NT)
        largest = jnp.max(scores, axis=1, keepdims=True)
        e = jnp.exp2(scores - largest).astype(bf16)
        e_ref[:, i * WIN : (i + 1) * WIN] = e
        both = dot(e, v * own_b + (1 - own_b), NN)
        total = total + jnp.where(own, both, 0.0)
        sums = sums + jnp.where(nxt, both, 0.0)
    return total, pltpu.roll(sums, 96, 1)


def delta_parts(d_mixed, mixed, sums):
    blk_r = lax.broadcasted_iota(jnp.int32, (HALF, HALF), 0) >> 5
    blk_c = lax.broadcasted_iota(jnp.int32, (HALF, HALF), 1) >> 5
    same = (blk_c == blk_r).astype(f32).astype(bf16)
    _, l32 = lanes()
    product = d_mixed * mixed
    high = product.astype(bf16)
    low = (product - high.astype(f32)).astype(bf16)
    over = 1.0 / sums
    delta = pltpu.roll(-(dot(high, same, NN) + dot(low, same, NN)) * over, 32, 1)
    high = delta.astype(bf16).astype(f32)
    extra = jnp.where(l32 == 0, high, jnp.where(l32 == 1, delta - high, 0.0)).astype(bf16)
    return d_mixed * over, extra


def attend_back_heads(heads, e_ref, q_t, k, v, d_own, d_own_t, extra, dk_ref, dv_ref, base):
    d_q = 0.0
    for i, j in enumerate(heads):
        _, _, own_b, nxt_b = head_masks(j)
        e = e_ref[:, i * WIN : (i + 1) * WIN]
        d_weights = dot(d_own * own_b + extra * nxt_b, v * own_b + (1 - own_b), NT)
        d_scores = e * d_weights.astype(bf16)
        rows = slice(i * 32, (i + 1) * 32)
        dst = pl.ds(pl.multiple_of(base + i * 32, 32), 32)
        dv_ref[dst, :] = dot(d_own_t[rows], e, NN).astype(bf16)
        dk_ref[dst, :] = (dot(q_t[rows], d_scores, NN) * LN2).astype(bf16)
        d_q = d_q + dot(d_scores, k * own_b, NN)
    return d_q * SCALE


def weight_grads(normed, dq_ref, dk_ref, dv_ref, put):
    for g in range(2):
        put(g * HALF, dot(normed, dq_ref[g], TN))
    put(C, dot(dk_ref[...], normed, NN).T)
    put(2 * C, dot(dv_ref[...], normed, NN).T)


def input_grad(x, gain, wq_ref, dq_ref, dk_ref, dv_ref, dy):
    xhat, rstd = norm_parts(x)
    d_normed = jnp.zeros((WIN, C), f32)
    for g in range(2):
        d_normed = d_normed + dot(dq_ref[g], wq_ref[:, g * HALF : (g + 1) * HALF], NT)
    for part, ref in ((1, dk_ref), (2, dv_ref)):
        w_t = wq_ref[:, part * C : (part + 1) * C].astype(f32).T.astype(bf16)
        d_normed = d_normed + dot(ref[...], w_t, TN)
    d_hat = d_normed * gain
    mean_d = jnp.mean(d_hat, axis=-1, keepdims=True)
    mean_dx = jnp.mean(d_hat * xhat, axis=-1, keepdims=True)
    return dy.astype(f32) + rstd * (d_hat - mean_d - xhat * mean_dx)


def near_valid(n):
    i = lax.broadcasted_iota(jnp.int32, (WIN, 1), 0)
    return ((i & (PIECE - 1)) * SPLIT + (i >> 7)) < n


def split_into(tmp, read, write):
    for g in range(2):
        tmp[g] = read(slice(g * HALF, (g + 1) * HALF))
    for g in range(2):
        for f in range(SPLIT):
            write(f, slice(g * HALF, (g + 1) * HALF), tmp[g, pl.ds(f, PIECE, stride=SPLIT), :].astype(bf16))


def merge_into(tmp, read, out_ref):
    for g in range(2):
        for f in range(SPLIT):
            tmp[g, pl.ds(f, PIECE, stride=SPLIT), :] = read(slice(f * PIECE, (f + 1) * PIECE), slice(g * HALF, (g + 1) * HALF))
    for g in range(2):
        out_ref[:, g * HALF : (g + 1) * HALF] = tmp[g].astype(bf16)


def near_forward_kernel(
    n_ref, x_ref, cot_ref, gain_ref, wq_ref, wo_ref, out_ref, xp_out, normed_out, qkv_out, mixed_ref, sums_ref, e_out, tmp, acc, exq, exk, xp_ref, normed_ref, qkv_ref, e_s, sem
):
    step = pl.program_id(0)
    early = [
        pltpu.make_async_copy(src, dst, sem.at[2 + i])
        for i, (src, dst) in enumerate(((xp_ref, xp_out), (normed_ref, normed_out), (qkv_ref, qkv_out)))
    ]

    def save(i):
        slot = i & 1
        cols = pl.ds(pl.multiple_of(i * 2 * WIN, 2 * WIN), 2 * WIN)
        return pltpu.make_async_copy(e_s.at[slot], e_out.at[:, cols], sem.at[slot])

    @pl.when(step == 0)
    def _():
        def put_x(f, cols, piece):
            xp_ref[f * PIECE : (f + 1) * PIECE, cols] = piece

        split_into(tmp, lambda cols: x_ref[:, cols].astype(f32), put_x)
        xhat, _ = norm_parts(xp_ref[...].astype(f32))
        normed_ref[...] = (xhat * gain_ref[0:1, :]).astype(bf16)
        project(normed_ref[...], wq_ref, qkv_ref)
        for copy in early:
            copy.start()
        exq[...], exk[...] = group_extras(near_valid(n_ref[0]))

        def put_cot(f, cols, piece):
            out_ref[f * PIECE : (f + 1) * PIECE, C + cols.start : C + cols.stop] = piece

        kept = lax.broadcasted_iota(jnp.int32, (WIN, 1), 0) < n_ref[0]
        split_into(tmp, lambda cols: jnp.where(kept, cot_ref[:, cols].astype(f32), 0.0), put_cot)

    @pl.when(step >= 2)
    def _():
        save(step - 2).wait()

    g = step >> 1
    first = (step & 1) * 2
    total, sums = attend_heads(
        (first, first + 1), qkv_ref[g], qkv_ref[2 + g], qkv_ref[4 + g], exq[...], exk[...], e_s.at[step & 1]
    )
    save(step).start()

    @pl.when(first == 0)
    def _():
        acc[g, :, :HALF] = total
        acc[g, :, HALF:] = sums

    @pl.when(first != 0)
    def _():
        acc[g, :, :HALF] = acc[g, :, :HALF] + total
        acc[g, :, HALF:] = acc[g, :, HALF:] + sums

    @pl.when(step == 3)
    def _():
        y = xp_ref[...].astype(f32)
        for g in range(2):
            sums = acc[g, :, HALF:]
            sums_ref[g] = sums
            mixed = (acc[g, :, :HALF] / sums).astype(bf16)
            mixed_ref[g] = mixed
            y = y + dot(mixed, wo_ref[g * HALF : (g + 1) * HALF, :], NN)
        out_ref[:, :C] = y.astype(bf16)
        for copy in early:
            copy.wait()
        save(2).wait()
        save(3).wait()


def far_kernel(
    n_ref, in_ref, gain_ref, wq_ref, wo_ref, out_ref, mixed_s, dq, dk, dv, qkv, dmix, e_s, exq, exk
):
    def valid():
        return lax.broadcasted_iota(jnp.int32, (WIN, 1), 0) < n_ref[0]

    xhat, _ = norm_parts(in_ref[:, :C].astype(f32))
    project((xhat * gain_ref[1:2, :]).astype(bf16), wq_ref, qkv)
    exq[...], exk[...] = group_extras(valid())
    d_mixed = dot(in_ref[:, C:], wo_ref[...], NT).astype(bf16)
    for i in range(2):
        dmix[i] = d_mixed[:, i * HALF : (i + 1) * HALF]

    for g in range(2):
        q, k, v = qkv[g], qkv[2 + g], qkv[4 + g]
        total, sums = attend_heads(range(4), q, k, v, exq[...], exk[...], e_s)
        mixed = total / sums
        mixed_s[g] = mixed.astype(bf16)
        d_own, extra = delta_parts(dmix[g].astype(f32), mixed, sums)
        d_q = attend_back_heads(
            range(4), e_s, q.astype(f32).T.astype(bf16), k, v, d_own.astype(bf16), d_own.T.astype(bf16), extra, dk, dv, g * HALF
        )
        dq[g] = d_q.astype(bf16)

    x = in_ref[:, :C].astype(f32)
    y = x
    for i in range(2):
        y = y + dot(mixed_s[i], wo_ref[i * HALF : (i + 1) * HALF, :], NN)
    out_ref[:, C:] = jnp.where(valid(), y, 0.0).astype(bf16)
    out_ref[:, :C] = input_grad(x, gain_ref[1:2, :], wq_ref, dq, dk, dv, in_ref[:, C:]).astype(bf16)


def far_grads_kernel(in_ref, gain_ref, mixed_ref, dq, dk, dv, pay_ref):
    def put(col, piece):
        pay_ref[:, col : col + piece.shape[1]] = piece.astype(bf16)

    for i in range(2):
        pay_ref[i * HALF : (i + 1) * HALF, 768:1024] = dot(mixed_ref[i], in_ref[:, C:], TN).astype(bf16)
    xhat, _ = norm_parts(in_ref[:, :C].astype(f32))
    weight_grads((xhat * gain_ref[1:2, :]).astype(bf16), dq, dk, dv, put)


def near_finish_kernel(in_ref, xp_ref, gain_ref, wq_ref, dq, dk, dv, dx_ref, res_ref, tmp):
    merge_into(tmp, lambda rows, cols: in_ref[rows, C + cols.start : C + cols.stop].astype(f32), res_ref)
    dx = input_grad(xp_ref[...].astype(f32), gain_ref[0:1, :], wq_ref, dq, dk, dv, in_ref[:, :C])
    merge_into(tmp, lambda rows, cols: dx[rows, cols], dx_ref)


def near_backward_kernel(
    core_ref,
    in_ref,
    normed_ref,
    wo_ref,
    qkv_ref,
    mixed_ref,
    sums_ref,
    two_ref,
    e_ref,
    keep_ref,
    send_ref,
    dq,
    dk,
    dv,
    pay_ref,
    down,
    down_t,
    q_t,
    extra_s,
    e_s,
    sem,
):
    step = pl.program_id(0)

    def put(col, piece):
        pay_ref[:, col : col + piece.shape[1]] = piece.astype(bf16)

    def fetch(i):
        cols = pl.ds(pl.multiple_of(i * 4 * WIN, 4 * WIN), 4 * WIN)
        return pltpu.make_async_copy(e_ref.at[:, cols], e_s.at[i], sem.at[i])

    @pl.when(step == 0)
    def _():
        fetch(0).start()
        fetch(1).start()
        dy = in_ref[:, :C]
        d_mixed = dot(dy, wo_ref[...], NT).astype(bf16).astype(f32)
        for i in range(2):
            rows = slice(i * HALF, (i + 1) * HALF)
            d_own, extra = delta_parts(d_mixed[:, rows], mixed_ref[i].astype(f32), sums_ref[i])
            down[i] = d_own.astype(bf16)
            down_t[rows, :] = d_own.T.astype(bf16)
            q_t[rows, :] = qkv_ref[i].astype(f32).T.astype(bf16)
            extra_s[i] = extra
            pay_ref[rows, 768:1024] = dot(mixed_ref[i], dy, TN).astype(bf16)
        pay_ref[:, 1024:2048] = two_ref[...]

    fetch(step).wait()
    g = step
    base = pl.multiple_of(step * HALF, HALF)
    d_q = attend_back_heads(
        range(4),
        e_s.at[step],
        q_t[pl.ds(base, HALF), :],
        qkv_ref[2 + g],
        qkv_ref[4 + g],
        down[g],
        down_t[pl.ds(base, HALF), :],
        extra_s[g],
        dk,
        dv,
        base,
    )

    dq[g] = d_q.astype(bf16)

    @pl.when(step == 1)
    def _():
        weight_grads(normed_ref[...], dq, dk, dv, put)
        core = core_ref[0]
        keep_ref[...] = pay_ref[pl.ds(pl.multiple_of(core * HALF, HALF), HALF), :]
        send_ref[...] = pay_ref[pl.ds(pl.multiple_of((1 - core) * HALF, HALF), HALF), :]


def spread_kernel(core_ref, mine_ref, other_ref, gain_ref, wq_ref, gains_ref, qkv_ref, proj_ref):
    core = core_ref[0]
    for ref, half in ((mine_ref, core), (other_ref, 1 - core)):
        rows = pl.ds(pl.multiple_of(half * HALF, HALF), HALF)
        for b in range(2):
            qkv_ref[b, rows, :] = ref[:, b * 1024 : b * 1024 + 768].astype(f32)
            proj_ref[b, rows, :] = ref[:, b * 1024 + 768 : (b + 1) * 1024].astype(f32)
    for b in range(2):
        along = jnp.sum(qkv_ref[b] * wq_ref[b].astype(f32), axis=1, keepdims=True)
        gains_ref[b : b + 1, :] = jnp.broadcast_to(along, (C, HALF)).T[:1] / gain_ref[b : b + 1, :]


def layer(shape, which):
    return pl.BlockSpec((None,) + shape, lambda i: (which, 0, 0))


def spec(shape):
    return pl.BlockSpec(shape, lambda i: (0,) * len(shape))


SCALAR = pl.BlockSpec(memory_space=pltpu.SMEM)
ANY = pl.BlockSpec(memory_space=pl.ANY)
PARAMS = pltpu.CompilerParams(vmem_limit_bytes=LIMIT)
ROWS = (WIN, C)
PAIR_ROWS = (WIN, 2 * C)
SPLIT_ROWS = (2, WIN, HALF)


def sds(shape, dtype):
    return jax.ShapeDtypeStruct(shape, dtype)


def cost(products):
    return pl.CostEstimate(flops=products * HEADS * 2 * WIN * WIN * HALF, bytes_accessed=2**24, transcendentals=2**23)


def near_forward(n, x, cot, gain, wq, wo):
    return pl.pallas_call(
        near_forward_kernel,
        grid=(4,),
        in_specs=[SCALAR, spec(ROWS), spec(ROWS), spec((2, C)), layer((C, 3 * C), 0), layer((C, C), 0)],
        out_specs=[spec(PAIR_ROWS), ANY, ANY, ANY, spec(SPLIT_ROWS), spec(SPLIT_ROWS), ANY],
        out_shape=[
            sds(PAIR_ROWS, bf16),
            sds(ROWS, bf16),
            sds(ROWS, bf16),
            sds((6, WIN, HALF), bf16),
            sds(SPLIT_ROWS, bf16),
            sds(SPLIT_ROWS, f32),
            sds((WIN, HEADS * WIN), bf16),
        ],
        scratch_shapes=[
            pltpu.VMEM(SPLIT_ROWS, f32),
            pltpu.VMEM((2, WIN, C), f32),
            pltpu.VMEM((WIN, HALF), bf16),
            pltpu.VMEM((WIN, HALF), bf16),
            pltpu.VMEM(ROWS, bf16),
            pltpu.VMEM(ROWS, bf16),
            pltpu.VMEM((6, WIN, HALF), bf16),
            pltpu.VMEM((2, WIN, 2 * WIN), bf16),
            pltpu.SemaphoreType.DMA((5,)),
        ],
        compiler_params=PARAMS,
        cost_estimate=cost(2),
        name="near_forward",
    )(n, x, cot, gain, wq, wo)


D_ROWS = [SPLIT_ROWS, (C, WIN), (C, WIN)]
D_SHAPES = [sds(shape, bf16) for shape in D_ROWS]
D_SPECS = [spec(shape) for shape in D_ROWS]


def far_both(n, rows, gain, wq, wo):
    return pl.pallas_call(
        far_kernel,
        grid=(1,),
        in_specs=[SCALAR, spec(PAIR_ROWS), spec((2, C)), layer((C, 3 * C), 1), layer((C, C), 1)],
        out_specs=[spec(PAIR_ROWS), spec(SPLIT_ROWS), *D_SPECS],
        out_shape=[sds(PAIR_ROWS, bf16), sds(SPLIT_ROWS, bf16), *D_SHAPES],
        scratch_shapes=[
            pltpu.VMEM((6, WIN, HALF), bf16),
            pltpu.VMEM(SPLIT_ROWS, bf16),
            pltpu.VMEM((WIN, 4 * WIN), bf16),
            pltpu.VMEM((WIN, HALF), bf16),
            pltpu.VMEM((WIN, HALF), bf16),
        ],
        compiler_params=PARAMS,
        cost_estimate=cost(6),
        name="far_both",
    )(n, rows, gain, wq, wo)


def far_grads(rows, gain, mixed, dq, dk, dv):
    return pl.pallas_call(
        far_grads_kernel,
        grid=(1,),
        in_specs=[spec(PAIR_ROWS), spec((2, C)), spec(SPLIT_ROWS), *D_SPECS],
        out_specs=spec((C, 1024)),
        out_shape=sds((C, 1024), bf16),
        compiler_params=PARAMS,
        cost_estimate=pl.CostEstimate(flops=2**30, bytes_accessed=2**22, transcendentals=0),
        name="far_grads",
    )(rows, gain, mixed, dq, dk, dv)


def near_finish(rows, xp, gain, wq, dq, dk, dv):
    return pl.pallas_call(
        near_finish_kernel,
        grid=(1,),
        in_specs=[spec(PAIR_ROWS), spec(ROWS), spec((2, C)), layer((C, 3 * C), 0), *D_SPECS],
        out_specs=[spec(ROWS), spec(ROWS)],
        out_shape=[sds(ROWS, bf16), sds(ROWS, bf16)],
        scratch_shapes=[pltpu.VMEM(SPLIT_ROWS, f32)],
        compiler_params=PARAMS,
        cost_estimate=pl.CostEstimate(flops=2**30, bytes_accessed=2**22, transcendentals=0),
        name="near_finish",
    )(rows, xp, gain, wq, dq, dk, dv)


def near_backward(core, rows, normed, wo, qkv, mixed, sums, two, e):
    return pl.pallas_call(
        near_backward_kernel,
        grid=(2,),
        in_specs=[
            SCALAR,
            spec(PAIR_ROWS),
            spec(ROWS),
            layer((C, C), 0),
            spec((6, WIN, HALF)),
            spec(SPLIT_ROWS),
            spec(SPLIT_ROWS),
            spec((C, 1024)),
            pl.BlockSpec(memory_space=pl.ANY),
        ],
        out_specs=[spec((HALF, 2048)), spec((HALF, 2048)), *D_SPECS],
        out_shape=[sds((HALF, 2048), bf16), sds((HALF, 2048), bf16), *D_SHAPES],
        scratch_shapes=[
            pltpu.VMEM((C, 2048), bf16),
            pltpu.VMEM(SPLIT_ROWS, bf16),
            pltpu.VMEM((C, WIN), bf16),
            pltpu.VMEM((C, WIN), bf16),
            pltpu.VMEM(SPLIT_ROWS, bf16),
            pltpu.VMEM((2, WIN, 4 * WIN), bf16),
            pltpu.SemaphoreType.DMA((2,)),
        ],
        compiler_params=PARAMS,
        cost_estimate=cost(4),
        name="near_backward",
    )(core, rows, normed, wo, qkv, mixed, sums, two, e)


def spread(core, mine, other, gain, wq):
    vmem = pl.BlockSpec(memory_space=pltpu.VMEM)
    return pl.pallas_call(
        spread_kernel,
        in_specs=[SCALAR, vmem, vmem, vmem, vmem],
        out_shape=[sds((2, C), f32), sds((2, C, 3 * C), f32), sds((2, C, C), f32)],
        compiler_params=PARAMS,
        name="spread",
    )(core, mine, other, gain, wq)


def exchange(rows, axis, groups=None):
    return lax.all_to_all(rows, axis, split_axis=0, concat_axis=0, tiled=True, axis_index_groups=groups)


def sum_everywhere(keep, send, factor, beside):
    scenes, groups = lax.axis_size("scene"), lax.axis_size("seq")
    width = keep.shape[1]
    pair = [(i, i ^ 1) for i in range(groups)]
    chips = [list(range(core, groups, 2)) for core in range(2)]
    many = groups // 2
    part = (keep.astype(f32) + lax.ppermute(send, "seq", pair).astype(f32)).astype(bf16)
    part = exchange(part.reshape(many, scenes, width), "seq", chips)
    part, beside = lax.optimization_barrier((part, beside))
    part = jnp.sum(part.astype(f32), axis=0)
    part = exchange(part.astype(bf16).reshape(scenes, 1, width), "scene").astype(f32)
    row = (jnp.sum(part, axis=0, keepdims=True) * factor).astype(bf16)
    rows = exchange(jnp.broadcast_to(row, (scenes, 1, width)), "scene").reshape(1, scenes, width)
    mine = exchange(jnp.broadcast_to(rows, (many, scenes, width)), "seq", chips).reshape(HALF, width)
    return mine, lax.ppermute(mine, "seq", pair), beside


def body(x_in, counts, ln_gains, w_qkv, w_proj, cotangent):
    groups = lax.axis_size("seq")
    place = lax.axis_index("seq")
    factor = (WIN * lax.axis_size("scene") * groups) ** (-0.5)
    n_near = counts - place * WIN
    n_far = (counts - place + groups - 1) // groups

    def swap(rows):
        return exchange(rows.reshape(SPLIT, PIECE, 2 * C), "seq").reshape(PAIR_ROWS)

    core = jnp.full((1,), place % 2, jnp.int32)
    first, xp, normed, qkv, mixed, sums, e = near_forward(n_near, x_in, cotangent, ln_gains, w_qkv, w_proj)
    rows_far = swap(first)
    back, *far_parts = far_both(n_far, rows_far, ln_gains, w_qkv, w_proj)
    rows = swap(back)
    two = far_grads(rows_far, ln_gains, *far_parts)
    keep, send, *d_rows = near_backward(core, rows, normed, w_proj, qkv, mixed, sums, two, e)
    beside = near_finish(rows, xp, ln_gains, w_qkv, *d_rows)
    mine, other, (d_input, result) = sum_everywhere(keep, send, factor, tuple(beside))
    gains, grads, projs = spread(core, mine, other, ln_gains, w_qkv)
    return result, d_input, gains, grads, projs


def solution(mesh):
    in_specs = (P(("scene", "seq"), None), P("scene"), P(), P(), P(), P(("scene", "seq"), None))
    out_specs = (P(("scene", "seq"), None), P(("scene", "seq"), None), P(), P(), P())
    return jax.shard_map(body, mesh=mesh, in_specs=in_specs, out_specs=out_specs, check_vma=False)
```
